32 devices in a mesh: rep: 2 (over y), wide: 16 (over z, x, core).
Axes of the slice: x: 2, y: 2, z: 4, core: 2. Of those that a mesh axis runs over, the one named last changes fastest.
Arguments:
- normed_hidden: bfloat16 [4096, 8192], P(('rep', 'wide')), parts along dimension 0, may hold values from -6 to 6
- fresh_queries: bfloat16 [4096, 1024], P(('rep', 'wide')), parts along dimension 0, may hold values from -48 to 48
- fresh_key_value: bfloat16 [4096, 256], P(('rep', 'wide')), parts along dimension 0, may hold values from -6 to 6
- key_value_cache: bfloat16 [4096, 64, 256], P(('rep', 'wide')), parts along dimension 0, may hold values from -16 to 16
- lengths: int32 [4096], P(('rep', 'wide')), parts along dimension 0, may hold values from 2 to 64, as said below
- adapter_choice: int32 [4096], P(('rep', 'wide')), parts along dimension 0, may hold values from 0 to 63, as said below
- low_rank_down: bfloat16 [64, 8192, 128], P('wide'), may hold values from -0.0625 to 0.0625
- low_rank_up: bfloat16 [64, 2, 64, 128], P('wide'), may hold values from -0.75 to 0.75
Outputs:
- new_entry: bfloat16 [4096, 256], P(('rep', 'wide')), parts along dimension 0
- attended: bfloat16 [4096, 1024], P(('rep', 'wide')), parts along dimension 0
The draws below stay inside these ranges and needn't reach their ends.
There are 2 independent parts, one for each index of `rep`. The reference program is written for one: setup_inputs(seed, part) draws one part's arguments, and reference() takes and returns one part's arrays. A program takes and returns all parts, laid end to end along the dimension named above; an argument that names none is the same for every part. Nothing has to cross between parts.
Inputs may be any that keep to these rules, and one draw needn't show every extreme that they name: `adapter_choice`: adapter a is stored on index a // 4 of wide. Among the rows of one device at most 16 name adapters stored on one device, and in every draw the adapters of some device are named by exactly 16 rows of every device. `lengths`: some request uses all 64 positions.
All inputs are finite; a program needn't handle non-finite values.
Results may differ from the reference program's by a relative error of at most 0.0063.
Values may be sent and summed in bfloat16 or wider, within the bound.
A program may use at most 64 MiB of HBM per device.

```python
import math
import jax
import jax.numpy as jnp
from jax import lax

MODEL_WIDTH = 8192
HEAD_SIZE = 128
QH = 8
ADAPTER_RANK = 64
ADP_DEV = 4
REQ_DEV = 128
CTX = 64
ADAPTER_TOTAL = 64
REQS = 2048
CAP = 16
N_WIDE = 16


def draw_key_value_cache(key, part):
    key = jax.random.fold_in(key, 5)
    cache = jax.random.truncated_normal(key, -5.0, 5.0, (REQS, CTX, 2 * HEAD_SIZE), jnp.float32)
    return cache.astype(jnp.bfloat16)


def draw_fresh_queries(key, part):
    key = jax.random.fold_in(key, 7)
    queries = jax.random.truncated_normal(key, -5.0, 5.0, (REQS, QH * HEAD_SIZE), jnp.float32)
    return queries.astype(jnp.bfloat16)


def draw_lengths(key, part):
    key = jax.random.fold_in(key, 9)
    drawn = jax.random.randint(key, (REQS,), 2, CTX + 1, dtype=jnp.int32)
    return drawn.at[0].set(CTX)


def draw_adapter_choice(key, part):
    key = jax.random.fold_in(key, 3)
    keys = jax.random.split(key, 5)
    slots = N_WIDE * CAP
    hottest = jax.random.randint(keys[0], (), 0, N_WIDE, dtype=jnp.int32)
    appeal = jax.random.randint(keys[1], (N_WIDE,), 1, 9, dtype=jnp.int32)
    slot_owner = jnp.arange(slots, dtype=jnp.int32) // CAP
    noise = jax.random.randint(keys[2], (N_WIDE, slots), 0, 16384, dtype=jnp.int32)
    scores = noise * appeal[slot_owner][None, :] * slots + jnp.arange(slots, dtype=jnp.int32)[None, :]
    scores = scores + jnp.where(slot_owner == hottest, 2 ** 30, 0)[None, :]
    _, picked = lax.top_k(scores, REQ_DEV)
    owner = picked // CAP
    within = jax.random.randint(keys[3], (N_WIDE, REQ_DEV), 0, ADP_DEV, dtype=jnp.int32)
    chosen_ids = owner * ADP_DEV + within
    shuffle = jax.random.randint(keys[4], (N_WIDE, REQ_DEV), 0, 2 ** 20, dtype=jnp.int32) * REQ_DEV
    shuffle = shuffle + jnp.arange(REQ_DEV, dtype=jnp.int32)[None, :]
    order = jnp.argsort(shuffle, axis=1)
    return jnp.take_along_axis(chosen_ids, order, axis=1).reshape(REQS).astype(jnp.int32)


def level_of(key, extent, pieces, low, largest):
    def one(axis_at, shards_of):
        draws = jax.random.uniform(jax.random.fold_in(jax.random.fold_in(key, 6), axis_at), (shards_of,), jnp.float32, low / len(pieces), largest / len(pieces))
        return jnp.repeat(jnp.exp(draws), extent[axis_at] // shards_of).reshape((-1,) + (1,) * (len(extent) - axis_at - 1))

    gain = one(*pieces[0])
    for cut in pieces[1:]:
        gain = gain * one(*cut)
    return gain


def bell_draw(key, extent, width, limit, cuts=(), held_as=jnp.bfloat16):
    factor_of = level_of(key, extent, cuts, -0.22, 0.18) if cuts else 1.0
    array = jax.random.normal(key, extent, jnp.float32) * width * factor_of
    return jnp.minimum(jnp.maximum(array, -limit), limit).astype(held_as)


def setup_inputs(seed: int = 0, part: int = 0) -> dict:
    key_list = jax.random.split(jax.random.key(seed), 9)
    part_keys = jax.random.split(jax.random.fold_in(key_list[8], part), 9)
    normed_hidden = bell_draw(part_keys[0], (REQS, MODEL_WIDTH), 1.0, 6.0, ((0, 16),))
    fresh_queries = draw_fresh_queries(jax.random.fold_in(jax.random.fold_in(key_list[8], part), 71), part)
    fresh_key_value = bell_draw(part_keys[2], (REQS, 2 * HEAD_SIZE), 1.0, 6.0, ((0, 16),))
    key_value_cache = draw_key_value_cache(jax.random.fold_in(jax.random.fold_in(key_list[8], part), 71), part)
    lengths = draw_lengths(jax.random.fold_in(jax.random.fold_in(key_list[8], part), 71), part)
    adapter_choice = draw_adapter_choice(jax.random.fold_in(jax.random.fold_in(key_list[8], part), 71), part)
    low_rank_down = bell_draw(key_list[6], (ADAPTER_TOTAL, MODEL_WIDTH, 2 * ADAPTER_RANK), MODEL_WIDTH ** -0.5, 0.0625, ((0, 16),))
    low_rank_up = bell_draw(key_list[7], (ADAPTER_TOTAL, 2, ADAPTER_RANK, HEAD_SIZE), ADAPTER_RANK ** -0.5, 0.75, ((0, 16),))
    return dict(normed_hidden=normed_hidden, fresh_queries=fresh_queries, fresh_key_value=fresh_key_value, key_value_cache=key_value_cache, lengths=lengths, adapter_choice=adapter_choice, low_rank_down=low_rank_down, low_rank_up=low_rank_up)


def low_rank_block(hidden_state_rows, adapter_index_rows, low_rank_down, low_rank_up):
    count_rows = hidden_state_rows.shape[0]
    down_factor_rows = low_rank_down[adapter_index_rows].astype(jnp.float32)
    project_input = jnp.einsum('bd,bdr->br', hidden_state_rows.astype(jnp.float32), down_factor_rows)
    project_input = lax.optimization_barrier(project_input.astype(jnp.bfloat16)).astype(jnp.float32)
    up_factor_rows = low_rank_up[adapter_index_rows].astype(jnp.float32)
    low_rank_update = jnp.einsum('btr,btrh->bth', project_input.reshape(count_rows, 2, ADAPTER_RANK), up_factor_rows)
    return low_rank_update.reshape(count_rows, 2 * HEAD_SIZE).astype(jnp.bfloat16)

def attend_block(query_rows, cache_rows, length_rows, entry_rows):
    count_rows = query_rows.shape[0]
    queries = query_rows.astype(jnp.float32).reshape(count_rows, QH, HEAD_SIZE)
    cached_keys = cache_rows[:, :, :HEAD_SIZE].astype(jnp.float32)
    cached_values = cache_rows[:, :, HEAD_SIZE:].astype(jnp.float32)
    entry_float = entry_rows.astype(jnp.float32)
    scores = jnp.einsum('rqh,rch->rqc', queries, cached_keys) / math.sqrt(HEAD_SIZE)
    usable = (jnp.arange(CTX, dtype=jnp.int32)[None, :] < length_rows[:, None])[:, None, :]
    scores = jnp.where(usable, scores, -1e+30)
    fresh_score = jnp.einsum('rqh,rh->rq', queries, entry_float[:, :HEAD_SIZE]) / math.sqrt(HEAD_SIZE)
    highest = jnp.maximum(lax.optimization_barrier(jnp.max(scores, axis=2)), fresh_score)
    cached_exp = jnp.where(usable, jnp.exp(scores - highest[:, :, None]), 0.0)
    fresh_exp = jnp.exp(fresh_score - highest)
    denominator = lax.optimization_barrier(jnp.sum(cached_exp, axis=2)) + fresh_exp
    cached_weight = lax.optimization_barrier((cached_exp / denominator[:, :, None]).astype(jnp.bfloat16))
    fresh_weight = lax.optimization_barrier((fresh_exp / denominator).astype(jnp.bfloat16))
    output = jnp.einsum('rqc,rch->rqh', cached_weight.astype(jnp.float32), cached_values)
    output = output + fresh_weight.astype(jnp.float32)[:, :, None] * entry_float[:, None, HEAD_SIZE:]
    return output.astype(jnp.bfloat16).reshape(count_rows, QH * HEAD_SIZE)

def reference(normed_hidden, fresh_queries, fresh_key_value, key_value_cache, lengths, adapter_choice, low_rank_down, low_rank_up):
    hidden_state_blocks = normed_hidden.reshape(N_WIDE, REQ_DEV, MODEL_WIDTH)
    adapter_index_blocks = adapter_choice.reshape(N_WIDE, REQ_DEV)
    low_rank_update = lax.map(lambda paired_rows: low_rank_block(paired_rows[0], paired_rows[1], low_rank_down, low_rank_up), (hidden_state_blocks, adapter_index_blocks))
    low_rank_update = lax.optimization_barrier(low_rank_update.reshape(REQS, 2 * HEAD_SIZE))
    new_entry = (fresh_key_value.astype(jnp.float32) + low_rank_update.astype(jnp.float32)).astype(jnp.bfloat16)
    grouped = (fresh_queries.reshape(N_WIDE, REQ_DEV, QH * HEAD_SIZE), key_value_cache.reshape(N_WIDE, REQ_DEV, CTX, 2 * HEAD_SIZE), lengths.reshape(N_WIDE, REQ_DEV), new_entry.reshape(N_WIDE, REQ_DEV, 2 * HEAD_SIZE))
    attended = lax.map(lambda group: attend_block(group[0], group[1], group[2], group[3]), grouped)
    return (new_entry, attended.reshape(REQS, QH * HEAD_SIZE))
```

```python
import functools
import math

import jax
import jax.numpy as jnp
from jax import lax
from jax.experimental import pallas as pl
from jax.experimental.pallas import tpu as pltpu
from jax.sharding import PartitionSpec as P

CHUNKS = 4


def apply_low_rank(received_rows, request_labels, low_rank_down, low_rank_up):
    kept_count = low_rank_down.shape[0]
    double_rank = low_rank_down.shape[2]
    senders = received_rows.shape[0]
    per_owner = received_rows.shape[1]
    picked = request_labels[:, :, None] == jnp.arange(kept_count)[None, None, :]
    project_input = jnp.einsum(
        "ikv,hvp->ikhp", received_rows, low_rank_down, preferred_element_type=jnp.float32
    ).astype(jnp.bfloat16)
    project_input = jnp.where(picked[:, :, :, None], project_input, jnp.zeros_like(project_input))
    project_input = project_input.reshape(senders, per_owner, kept_count, 2, double_rank // 2)
    low_rank_update = jnp.einsum(
        "uygwk,gwke->uywe", project_input, low_rank_up, preferred_element_type=jnp.float32
    )
    return low_rank_update.astype(jnp.bfloat16).reshape(senders, per_owner, -1)


def return_rows(low_rank_update):
    return lax.all_to_all(low_rank_update, "wide", split_axis=0, concat_axis=0, tiled=True)


def attend(fresh_queries, key_value_cache, lengths, entry):
    head_size = entry.shape[1] // 2
    requests = fresh_queries.shape[0]
    context = key_value_cache.shape[1]
    queries = fresh_queries.reshape(requests, -1, head_size)
    scores = jnp.einsum(
        "rqh,rch->rqc",
        queries,
        key_value_cache[:, :, :head_size],
        preferred_element_type=jnp.float32,
    ) / math.sqrt(head_size)
    usable = (jnp.arange(context, dtype=jnp.int32)[None, :] < lengths[:, None])[:, None, :]
    scores = jnp.where(usable, scores, -1e30)
    fresh_score = jnp.einsum(
        "rqh,rh->rq", queries, entry[:, :head_size], preferred_element_type=jnp.float32
    ) / math.sqrt(head_size)
    highest = jnp.maximum(jnp.max(scores, axis=2), fresh_score)
    cached_exp = jnp.where(usable, jnp.exp(scores - highest[:, :, None]), 0.0)
    fresh_exp = jnp.exp(fresh_score - highest)
    denominator = jnp.sum(cached_exp, axis=2) + fresh_exp
    cached_weight = (cached_exp / denominator[:, :, None]).astype(jnp.bfloat16)
    fresh_weight = (fresh_exp / denominator).astype(jnp.bfloat16)
    output = jnp.einsum(
        "rqc,rch->rqh",
        cached_weight,
        key_value_cache[:, :, head_size:],
        preferred_element_type=jnp.float32,
    )
    output = output + fresh_weight.astype(jnp.float32)[:, :, None] * entry[
        :, None, head_size:
    ].astype(jnp.float32)
    return output.astype(jnp.bfloat16).reshape(requests, -1)


def shards(
    normed_hidden,
    fresh_queries,
    fresh_key_value,
    key_value_cache,
    lengths,
    adapter_choice,
    low_rank_down,
    low_rank_up,
):
    devices_wide = lax.axis_size("wide")
    requests = normed_hidden.shape[0]
    per_owner = 2 * requests // devices_wide
    kept_count = low_rank_down.shape[0]
    owners = adapter_choice // kept_count
    owner_hit = owners[:, None] == jnp.arange(devices_wide, dtype=jnp.int32)[None, :]
    earlier = jnp.cumsum(owner_hit.astype(jnp.int32), axis=0) - 1
    position = jnp.sum(jnp.where(owner_hit, earlier, 0), axis=1)
    target = owners * per_owner + position
    placing = (
        target[:, None] == jnp.arange(devices_wide * per_owner, dtype=jnp.int32)[None, :]
    ).astype(jnp.bfloat16)
    packed = jnp.einsum(
        "rs,rd->sd", placing, normed_hidden, preferred_element_type=jnp.float32
    ).astype(jnp.bfloat16)
    packed = packed.reshape(devices_wide, per_owner, -1)
    every_id = lax.all_gather(adapter_choice, "wide", axis=0, tiled=True).reshape(
        devices_wide, requests
    )
    mine = every_id // kept_count == lax.axis_index("wide")
    order_mine = jnp.cumsum(mine.astype(jnp.int32), axis=1) - 1
    matched = mine[:, :, None] & (
        order_mine[:, :, None] == jnp.arange(per_owner, dtype=jnp.int32)[None, None, :]
    )
    request_labels = (
        jnp.sum(jnp.where(matched, (every_id % kept_count + 1)[:, :, None], 0), axis=1) - 1
    )
    received_rows = lax.all_to_all(packed, "wide", split_axis=0, concat_axis=0, tiled=True)
    returned_rows = return_rows(
        apply_low_rank(received_rows, request_labels, low_rank_down, low_rank_up)
    )
    flat_back = returned_rows.reshape(devices_wide * per_owner, -1)
    update_rows = jnp.einsum("rs,sh->rh", placing, flat_back, preferred_element_type=jnp.float32)
    new_entry = (fresh_key_value.astype(jnp.float32) + update_rows).astype(jnp.bfloat16)
    attended = attend(fresh_queries, key_value_cache, lengths, new_entry)
    return (new_entry, attended)

def wide_kernel(
    n,
    ids_ref,
    lengths_ref,
    hidden_ref,
    queries_ref,
    fresh_ref,
    cache_ref,
    down_ref,
    up_ref,
    entry_ref,
    attended_ref,
    hidden,
    cache,
    down,
    up,
    packed,
    received,
    labels_out,
    labels_in,
    update_out,
    update_in,
    placing,
    placing_t,
    queries,
    context_sum,
    highest,
    total,
    project,
    load_sem,
    self_sem,
    send_sem,
    recv_sem,
):
    chunks, per_owner, width = packed.shape[0], packed.shape[2], packed.shape[3]
    kept = up_ref.shape[0]
    rank = up_ref.shape[2]
    head = up_ref.shape[3]
    requests = ids_ref.shape[1]
    heads = queries.shape[1]
    slots = n * per_owner
    stride = 7 if n % 2 == 0 and n % 7 else 1
    me = lax.axis_index("wide")
    f32, bf16 = jnp.float32, jnp.bfloat16

    def columns(c):
        return pl.ds(pl.multiple_of(c * width, width), width)

    def hidden_load(c):
        return pltpu.make_async_copy(
            hidden_ref.at[:, columns(c)], hidden.at[c], load_sem.at[c]
        )

    def down_load(g):
        return pltpu.make_async_copy(
            down_ref.at[g], down.at[:, pl.ds(g * 2 * rank, 2 * rank)], load_sem.at[chunks + g]
        )

    cache_load = pltpu.make_async_copy(cache_ref, cache, load_sem.at[chunks + kept])

    for c in range(chunks):
        hidden_load(c).start()
    cache_load.start()
    for g in range(kept):
        down_load(g).start()

    barrier = pltpu.get_barrier_semaphore()

    @pl.loop(1, n)
    def _(k):
        pl.semaphore_signal(
            barrier,
            inc=1,
            device_id={"wide": lax.rem(me + k, n)},
            device_id_type=pl.DeviceIdType.MESH,
        )

    ids = ids_ref[...]
    adapter = lax.broadcasted_iota(jnp.int32, (n * kept, requests), 0)
    named = jnp.where(adapter == ids, 1.0, 0.0).astype(bf16)
    group_of = lax.broadcasted_iota(jnp.int32, (n, n * kept), 1)
    first = lax.broadcasted_iota(jnp.int32, (n, n * kept), 0) * kept
    grouping = jnp.where((group_of >= first) & (group_of < first + kept), 1.0, 0.0).astype(bf16)
    hit = jnp.dot(grouping, named, preferred_element_type=f32)
    before = lax.broadcasted_iota(jnp.int32, (requests, requests), 0)
    after = lax.broadcasted_iota(jnp.int32, (requests, requests), 1)
    earlier = jnp.dot(
        hit.astype(bf16),
        jnp.where(before < after, 1.0, 0.0).astype(bf16),
        preferred_element_type=f32,
    )
    position = jnp.where(hit > 0.5, earlier, -1.0).astype(jnp.int32)
    place = lax.broadcasted_iota(jnp.int32, (n, per_owner, requests), 1)
    chosen = jnp.where(place == position[:, None, :], 1.0, 0.0).reshape(slots, requests)
    placing[...] = chosen.astype(bf16)
    owner_row = jnp.sum(
        hit * lax.broadcasted_iota(jnp.int32, (n, requests), 0).astype(f32), axis=0, keepdims=True
    )
    within = ids - kept * owner_row.astype(jnp.int32)
    lane = lax.broadcasted_iota(jnp.int32, (128, requests), 0)
    flags = jnp.where(lane == within, 1.0, 0.0).astype(bf16)
    labels = lax.dot_general(
        placing[...], flags, (((1,), (1,)), ((), ())), preferred_element_type=f32
    )
    labels_out[...] = labels.astype(bf16).reshape(n, per_owner, 128)
    labels_in[me] = labels_out[me]

    pl.semaphore_wait(barrier, n - 1)

    def send(source, target, row, k):
        return pltpu.make_async_remote_copy(
            src_ref=source,
            dst_ref=target,
            send_sem=send_sem.at[row, k],
            recv_sem=recv_sem.at[row, k],
            device_id={"wide": lax.rem(me + k, n)},
            device_id_type=pl.DeviceIdType.MESH,
        )

    def row_copy(c, k):
        return send(packed.at[c, lax.rem(me + k, n)], received.at[c, me], c, k)

    def label_copy(k):
        return send(labels_out.at[lax.rem(me + k, n)], labels_in.at[me], chunks, k)

    def update_copy(k):
        return send(update_out.at[lax.rem(me + k, n)], update_in.at[me], chunks + 1, k)

    def self_copy(c):
        return pltpu.make_async_copy(packed.at[c, me], received.at[c, me], self_sem.at[c])

    step = min(width, 512)
    for c in range(chunks):
        hidden_load(c).wait()

        @pl.loop(0, width // step)
        def _(j):
            part = pl.ds(pl.multiple_of(j * step, step), step)
            rows = jnp.dot(placing[...], hidden[c, :, part], preferred_element_type=f32)
            packed[c, :, :, part] = rows.astype(bf16).reshape(n, per_owner, step)

        self_copy(c).start()

        @pl.loop(1, n)
        def _(j):
            row_copy(c, lax.rem(j * stride, n)).start()

        if c == 0:

            @pl.loop(1, n)
            def _(k):
                label_copy(k).start()

    placing_t[...] = chosen.T.astype(bf16)
    up[...] = jnp.zeros_like(up)
    for g in range(kept):
        for t in range(2):
            up[pl.ds((2 * g + t) * rank, rank), pl.ds(t * head, head)] = up_ref[g, t]
    for h in range(heads):
        queries[:, h, :] = queries_ref[:, pl.ds(h * head, head)].astype(f32)
    cache_load.wait()
    context = cache.shape[1]
    group = 8 if requests % 8 == 0 else 1

    @pl.loop(0, requests // group)
    def _(i):
        for u in range(group):
            r = i * group + u
            scores = lax.dot_general(
                queries[r].astype(bf16),
                cache[r, :, pl.ds(0, head)],
                (((1,), (1,)), ((), ())),
                preferred_element_type=f32,
            ) / math.sqrt(head)
            usable = lax.broadcasted_iota(jnp.int32, (heads, context), 1) < lengths_ref[r]
            scores = jnp.where(usable, scores, -1e30)
            top = jnp.max(scores, axis=1, keepdims=True)
            powers = jnp.where(usable, jnp.exp(scores - top), 0.0)
            highest[r] = jnp.broadcast_to(top, (heads, head))
            total[r] = jnp.broadcast_to(jnp.sum(powers, axis=1, keepdims=True), (heads, head))
            context_sum[r] = jnp.dot(
                powers.astype(bf16), cache[r, :, pl.ds(head, head)], preferred_element_type=f32
            )

    for g in range(kept):
        down_load(g).wait()

    for c in range(chunks):
        self_copy(c).wait()

        @pl.loop(1, n)
        def _(j):
            row_copy(c, lax.rem(j * stride, n)).wait_recv()

        product = jnp.dot(
            received[c].reshape(slots, width),
            down[pl.ds(c * width, width), :],
            preferred_element_type=f32,
        )
        if c == 0:
            project[...] = product
        else:
            project[...] += product

    @pl.loop(1, n)
    def _(k):
        label_copy(k).wait_recv()

    picked = labels_in[...].reshape(slots, 128).astype(f32)
    masked = [
        project[:, pl.ds(g * 2 * rank, 2 * rank)] * picked[:, g : g + 1] for g in range(kept)
    ]
    update = jnp.dot(
        jnp.concatenate(masked, axis=1).astype(bf16), up[...], preferred_element_type=f32
    )
    update_out[...] = update.astype(bf16).reshape(n, per_owner, 2 * head)

    @pl.loop(1, n)
    def _(k):
        update_copy(k).start()

    update_in[me] = update_out[me]

    @pl.loop(1, n)
    def _(k):
        update_copy(k).wait_recv()

    back = jnp.dot(
        placing_t[...], update_in[...].reshape(slots, 2 * head), preferred_element_type=f32
    )
    entry = (fresh_ref[...].astype(f32) + back).astype(bf16)
    entry_ref[...] = entry
    key = entry[:, :head].astype(f32)
    value = entry[:, head:].astype(f32)
    fresh_score = jnp.sum(queries[...] * key[:, None, :], axis=2, keepdims=True) / math.sqrt(head)
    old = highest[...]
    new = jnp.maximum(old, fresh_score)
    scale = jnp.exp(old - new)
    fresh_power = jnp.exp(fresh_score - new)
    context_sum[...] = (context_sum[...] * scale + fresh_power * value[:, None, :]) / (
        total[...] * scale + fresh_power
    )
    for h in range(heads):
        attended_ref[:, pl.ds(h * head, head)] = context_sum[:, h, :].astype(bf16)

    @pl.loop(1, n)
    def _(k):
        for c in range(chunks):
            row_copy(c, k).wait_send()
        label_copy(k).wait_send()
        update_copy(k).wait_send()


def fused(
    normed_hidden,
    fresh_queries,
    fresh_key_value,
    key_value_cache,
    lengths,
    adapter_choice,
    low_rank_down,
    low_rank_up,
):
    n = lax.axis_size("wide")
    requests, model = normed_hidden.shape
    per_owner = 2 * requests // n
    kept, _, double_rank = low_rank_down.shape
    head = low_rank_up.shape[3]
    heads = fresh_queries.shape[1] // head
    context = key_value_cache.shape[1]
    slots = n * per_owner
    chunks = CHUNKS
    width = model // chunks
    bf16, f32 = jnp.bfloat16, jnp.float32
    vmem = pl.BlockSpec(memory_space=pltpu.VMEM)
    smem = pl.BlockSpec(memory_space=pltpu.SMEM)
    anywhere = pl.BlockSpec(memory_space=pl.ANY)
    return pl.pallas_call(
        functools.partial(wide_kernel, n),
        out_shape=(
            jax.ShapeDtypeStruct((requests, 2 * head), bf16),
            jax.ShapeDtypeStruct((requests, heads * head), bf16),
        ),
        in_specs=[vmem, smem, anywhere, vmem, vmem, anywhere, anywhere, vmem],
        out_specs=(vmem, vmem),
        scratch_shapes=[
            pltpu.VMEM((chunks, requests, width), bf16),
            pltpu.VMEM((requests, context, 2 * head), bf16),
            pltpu.VMEM((model, kept * double_rank), bf16),
            pltpu.VMEM((kept * double_rank, 2 * head), bf16),
            pltpu.VMEM((chunks, n, per_owner, width), bf16),
            pltpu.VMEM((chunks, n, per_owner, width), bf16),
            pltpu.VMEM((n, per_owner, 128), bf16),
            pltpu.VMEM((n, per_owner, 128), bf16),
            pltpu.VMEM((n, per_owner, 2 * head), bf16),
            pltpu.VMEM((n, per_owner, 2 * head), bf16),
            pltpu.VMEM((slots, requests), bf16),
            pltpu.VMEM((requests, slots), bf16),
            pltpu.VMEM((requests, heads, head), f32),
            pltpu.VMEM((requests, heads, head), f32),
            pltpu.VMEM((requests, heads, head), f32),
            pltpu.VMEM((requests, heads, head), f32),
            pltpu.VMEM((slots, kept * double_rank), f32),
            pltpu.SemaphoreType.DMA((chunks + kept + 1,)),
            pltpu.SemaphoreType.DMA((chunks,)),
            pltpu.SemaphoreType.DMA((chunks + 2, n)),
            pltpu.SemaphoreType.DMA((chunks + 2, n)),
        ],
        compiler_params=pltpu.CompilerParams(
            collective_id=0, has_side_effects=True, vmem_limit_bytes=56 * 1024 * 1024
        ),
    )(
        adapter_choice.reshape(1, requests),
        lengths,
        normed_hidden,
        fresh_queries,
        fresh_key_value,
        key_value_cache,
        low_rank_down,
        low_rank_up,
    )


def device_step(*blocks):
    requests = blocks[0].shape[0]
    per_owner = 2 * requests // lax.axis_size("wide")
    if per_owner % 16:
        return shards(*blocks)
    return fused(*blocks)


def solution(mesh):
    return jax.shard_map(
        device_step,
        mesh=mesh,
        in_specs=(
            P(("rep", "wide"), None),
            P(("rep", "wide"), None),
            P(("rep", "wide"), None),
            P(("rep", "wide"), None, None),
            P(("rep", "wide")),
            P(("rep", "wide")),
            P("wide", None, None),
            P("wide", None, None, None),
        ),
        out_specs=(P(("rep", "wide"), None), P(("rep", "wide"), None)),
        check_vma=False,
    )
```

```python
import functools
import math

import jax
import jax.numpy as jnp
from jax import lax
from jax.experimental import pallas as pl
from jax.experimental.pallas import tpu as pltpu
from jax.sharding import PartitionSpec as P

CHUNKS = 4
HALF_CHUNKS = 8


def apply_low_rank(received_rows, request_labels, low_rank_down, low_rank_up):
    kept_count = low_rank_down.shape[0]
    double_rank = low_rank_down.shape[2]
    senders = received_rows.shape[0]
    per_owner = received_rows.shape[1]
    picked = request_labels[:, :, None] == jnp.arange(kept_count)[None, None, :]
    project_input = jnp.einsum(
        "ikv,hvp->ikhp", received_rows, low_rank_down, preferred_element_type=jnp.float32
    ).astype(jnp.bfloat16)
    project_input = jnp.where(picked[:, :, :, None], project_input, jnp.zeros_like(project_input))
    project_input = project_input.reshape(senders, per_owner, kept_count, 2, double_rank // 2)
    low_rank_update = jnp.einsum(
        "uygwk,gwke->uywe", project_input, low_rank_up, preferred_element_type=jnp.float32
    )
    return low_rank_update.astype(jnp.bfloat16).reshape(senders, per_owner, -1)


def return_rows(low_rank_update):
    return lax.all_to_all(low_rank_update, "wide", split_axis=0, concat_axis=0, tiled=True)


def attend(fresh_queries, key_value_cache, lengths, entry):
    head_size = entry.shape[1] // 2
    requests = fresh_queries.shape[0]
    context = key_value_cache.shape[1]
    queries = fresh_queries.reshape(requests, -1, head_size)
    scores = jnp.einsum(
        "rqh,rch->rqc",
        queries,
        key_value_cache[:, :, :head_size],
        preferred_element_type=jnp.float32,
    ) / math.sqrt(head_size)
    usable = (jnp.arange(context, dtype=jnp.int32)[None, :] < lengths[:, None])[:, None, :]
    scores = jnp.where(usable, scores, -1e30)
    fresh_score = jnp.einsum(
        "rqh,rh->rq", queries, entry[:, :head_size], preferred_element_type=jnp.float32
    ) / math.sqrt(head_size)
    highest = jnp.maximum(jnp.max(scores, axis=2), fresh_score)
    cached_exp = jnp.where(usable, jnp.exp(scores - highest[:, :, None]), 0.0)
    fresh_exp = jnp.exp(fresh_score - highest)
    denominator = jnp.sum(cached_exp, axis=2) + fresh_exp
    cached_weight = (cached_exp / denominator[:, :, None]).astype(jnp.bfloat16)
    fresh_weight = (fresh_exp / denominator).astype(jnp.bfloat16)
    output = jnp.einsum(
        "rqc,rch->rqh",
        cached_weight,
        key_value_cache[:, :, head_size:],
        preferred_element_type=jnp.float32,
    )
    output = output + fresh_weight.astype(jnp.float32)[:, :, None] * entry[
        :, None, head_size:
    ].astype(jnp.float32)
    return output.astype(jnp.bfloat16).reshape(requests, -1)


def shards(
    normed_hidden,
    fresh_queries,
    fresh_key_value,
    key_value_cache,
    lengths,
    adapter_choice,
    low_rank_down,
    low_rank_up,
):
    devices_wide = lax.axis_size("wide")
    requests = normed_hidden.shape[0]
    per_owner = 2 * requests // devices_wide
    kept_count = low_rank_down.shape[0]
    owners = adapter_choice // kept_count
    owner_hit = owners[:, None] == jnp.arange(devices_wide, dtype=jnp.int32)[None, :]
    earlier = jnp.cumsum(owner_hit.astype(jnp.int32), axis=0) - 1
    position = jnp.sum(jnp.where(owner_hit, earlier, 0), axis=1)
    target = owners * per_owner + position
    placing = (
        target[:, None] == jnp.arange(devices_wide * per_owner, dtype=jnp.int32)[None, :]
    ).astype(jnp.bfloat16)
    packed = jnp.einsum(
        "rs,rd->sd", placing, normed_hidden, preferred_element_type=jnp.float32
    ).astype(jnp.bfloat16)
    packed = packed.reshape(devices_wide, per_owner, -1)
    every_id = lax.all_gather(adapter_choice, "wide", axis=0, tiled=True).reshape(
        devices_wide, requests
    )
    mine = every_id // kept_count == lax.axis_index("wide")
    order_mine = jnp.cumsum(mine.astype(jnp.int32), axis=1) - 1
    matched = mine[:, :, None] & (
        order_mine[:, :, None] == jnp.arange(per_owner, dtype=jnp.int32)[None, None, :]
    )
    request_labels = (
        jnp.sum(jnp.where(matched, (every_id % kept_count + 1)[:, :, None], 0), axis=1) - 1
    )
    received_rows = lax.all_to_all(packed, "wide", split_axis=0, concat_axis=0, tiled=True)
    returned_rows = return_rows(
        apply_low_rank(received_rows, request_labels, low_rank_down, low_rank_up)
    )
    flat_back = returned_rows.reshape(devices_wide * per_owner, -1)
    update_rows = jnp.einsum("rs,sh->rh", placing, flat_back, preferred_element_type=jnp.float32)
    new_entry = (fresh_key_value.astype(jnp.float32) + update_rows).astype(jnp.bfloat16)
    attended = attend(fresh_queries, key_value_cache, lengths, new_entry)
    return (new_entry, attended)

def wide_kernel(
    n,
    ids_ref,
    lengths_ref,
    hidden_ref,
    queries_ref,
    fresh_ref,
    cache_ref,
    down_ref,
    up_ref,
    entry_ref,
    attended_ref,
    hidden,
    cache,
    down,
    up,
    packed,
    received,
    labels_out,
    labels_in,
    update_out,
    update_in,
    placing,
    placing_t,
    queries,
    context_sum,
    highest,
    total,
    project,
    load_sem,
    self_sem,
    send_sem,
    recv_sem,
):
    chunks, per_owner, width = packed.shape[0], packed.shape[2], packed.shape[3]
    kept = up_ref.shape[0]
    rank = up_ref.shape[2]
    head = up_ref.shape[3]
    requests = ids_ref.shape[1]
    heads = queries.shape[1]
    slots = n * per_owner
    stride = 7 if n % 2 == 0 and n % 7 else 1
    me = lax.axis_index("wide")
    f32, bf16 = jnp.float32, jnp.bfloat16

    def columns(c):
        return pl.ds(pl.multiple_of(c * width, width), width)

    def hidden_load(c):
        return pltpu.make_async_copy(
            hidden_ref.at[:, columns(c)], hidden.at[c], load_sem.at[c]
        )

    def down_load(g):
        return pltpu.make_async_copy(
            down_ref.at[g], down.at[:, pl.ds(g * 2 * rank, 2 * rank)], load_sem.at[chunks + g]
        )

    cache_load = pltpu.make_async_copy(cache_ref, cache, load_sem.at[chunks + kept])

    for c in range(chunks):
        hidden_load(c).start()
    cache_load.start()
    for g in range(kept):
        down_load(g).start()

    barrier = pltpu.get_barrier_semaphore()

    @pl.loop(1, n)
    def _(k):
        pl.semaphore_signal(
            barrier,
            inc=1,
            device_id={"wide": lax.rem(me + k, n)},
            device_id_type=pl.DeviceIdType.MESH,
        )

    ids = ids_ref[...]
    adapter = lax.broadcasted_iota(jnp.int32, (n * kept, requests), 0)
    named = jnp.where(adapter == ids, 1.0, 0.0).astype(bf16)
    group_of = lax.broadcasted_iota(jnp.int32, (n, n * kept), 1)
    first = lax.broadcasted_iota(jnp.int32, (n, n * kept), 0) * kept
    grouping = jnp.where((group_of >= first) & (group_of < first + kept), 1.0, 0.0).astype(bf16)
    hit = jnp.dot(grouping, named, preferred_element_type=f32)
    before = lax.broadcasted_iota(jnp.int32, (requests, requests), 0)
    after = lax.broadcasted_iota(jnp.int32, (requests, requests), 1)
    earlier = jnp.dot(
        hit.astype(bf16),
        jnp.where(before < after, 1.0, 0.0).astype(bf16),
        preferred_element_type=f32,
    )
    position = jnp.where(hit > 0.5, earlier, -1.0).astype(jnp.int32)
    place = lax.broadcasted_iota(jnp.int32, (n, per_owner, requests), 1)
    chosen = jnp.where(place == position[:, None, :], 1.0, 0.0).reshape(slots, requests)
    placing[...] = chosen.astype(bf16)
    owner_row = jnp.sum(
        hit * lax.broadcasted_iota(jnp.int32, (n, requests), 0).astype(f32), axis=0, keepdims=True
    )
    within = ids - kept * owner_row.astype(jnp.int32)
    lane = lax.broadcasted_iota(jnp.int32, (128, requests), 0)
    flags = jnp.where(lane == within, 1.0, 0.0).astype(bf16)
    labels = lax.dot_general(
        placing[...], flags, (((1,), (1,)), ((), ())), preferred_element_type=f32
    )
    labels_out[...] = labels.astype(bf16).reshape(n, per_owner, 128)
    labels_in[me] = labels_out[me]

    pl.semaphore_wait(barrier, n - 1)

    def send(source, target, row, k):
        return pltpu.make_async_remote_copy(
            src_ref=source,
            dst_ref=target,
            send_sem=send_sem.at[row, k],
            recv_sem=recv_sem.at[row, k],
            device_id={"wide": lax.rem(me + k, n)},
            device_id_type=pl.DeviceIdType.MESH,
        )

    def row_copy(c, k):
        return send(packed.at[c, lax.rem(me + k, n)], received.at[c, me], c, k)

    def label_copy(k):
        return send(labels_out.at[lax.rem(me + k, n)], labels_in.at[me], chunks, k)

    def update_copy(k):
        return send(update_out.at[lax.rem(me + k, n)], update_in.at[me], chunks + 1, k)

    def self_copy(c):
        return pltpu.make_async_copy(packed.at[c, me], received.at[c, me], self_sem.at[c])

    step = min(width, 512)
    for c in range(chunks):
        hidden_load(c).wait()

        @pl.loop(0, width // step)
        def _(j):
            part = pl.ds(pl.multiple_of(j * step, step), step)
            rows = jnp.dot(placing[...], hidden[c, :, part], preferred_element_type=f32)
            packed[c, :, :, part] = rows.astype(bf16).reshape(n, per_owner, step)

        self_copy(c).start()

        @pl.loop(1, n)
        def _(j):
            row_copy(c, lax.rem(j * stride, n)).start()

        if c == 0:

            @pl.loop(1, n)
            def _(k):
                label_copy(k).start()

    placing_t[...] = chosen.T.astype(bf16)
    up[...] = jnp.zeros_like(up)
    for g in range(kept):
        for t in range(2):
            up[pl.ds((2 * g + t) * rank, rank), pl.ds(t * head, head)] = up_ref[g, t]
    for h in range(heads):
        queries[:, h, :] = queries_ref[:, pl.ds(h * head, head)].astype(f32)
    cache_load.wait()
    context = cache.shape[1]
    group = 8 if requests % 8 == 0 else 1

    @pl.loop(0, requests // group)
    def _(i):
        for u in range(group):
            r = i * group + u
            scores = lax.dot_general(
                queries[r].astype(bf16),
                cache[r, :, pl.ds(0, head)],
                (((1,), (1,)), ((), ())),
                preferred_element_type=f32,
            ) / math.sqrt(head)
            usable = lax.broadcasted_iota(jnp.int32, (heads, context), 1) < lengths_ref[r]
            scores = jnp.where(usable, scores, -1e30)
            top = jnp.max(scores, axis=1, keepdims=True)
            powers = jnp.where(usable, jnp.exp(scores - top), 0.0)
            highest[r] = jnp.broadcast_to(top, (heads, head))
            total[r] = jnp.broadcast_to(jnp.sum(powers, axis=1, keepdims=True), (heads, head))
            context_sum[r] = jnp.dot(
                powers.astype(bf16), cache[r, :, pl.ds(head, head)], preferred_element_type=f32
            )

    for g in range(kept):
        down_load(g).wait()

    for c in range(chunks):
        self_copy(c).wait()

        @pl.loop(1, n)
        def _(j):
            row_copy(c, lax.rem(j * stride, n)).wait_recv()

        product = jnp.dot(
            received[c].reshape(slots, width),
            down[pl.ds(c * width, width), :],
            preferred_element_type=f32,
        )
        if c == 0:
            project[...] = product
        else:
            project[...] += product

    @pl.loop(1, n)
    def _(k):
        label_copy(k).wait_recv()

    picked = labels_in[...].reshape(slots, 128).astype(f32)
    masked = [
        project[:, pl.ds(g * 2 * rank, 2 * rank)] * picked[:, g : g + 1] for g in range(kept)
    ]
    update = jnp.dot(
        jnp.concatenate(masked, axis=1).astype(bf16), up[...], preferred_element_type=f32
    )
    update_out[...] = update.astype(bf16).reshape(n, per_owner, 2 * head)

    @pl.loop(1, n)
    def _(k):
        update_copy(k).start()

    update_in[me] = update_out[me]

    @pl.loop(1, n)
    def _(k):
        update_copy(k).wait_recv()

    back = jnp.dot(
        placing_t[...], update_in[...].reshape(slots, 2 * head), preferred_element_type=f32
    )
    entry = (fresh_ref[...].astype(f32) + back).astype(bf16)
    entry_ref[...] = entry
    key = entry[:, :head].astype(f32)
    value = entry[:, head:].astype(f32)
    fresh_score = jnp.sum(queries[...] * key[:, None, :], axis=2, keepdims=True) / math.sqrt(head)
    old = highest[...]
    new = jnp.maximum(old, fresh_score)
    scale = jnp.exp(old - new)
    fresh_power = jnp.exp(fresh_score - new)
    context_sum[...] = (context_sum[...] * scale + fresh_power * value[:, None, :]) / (
        total[...] * scale + fresh_power
    )
    for h in range(heads):
        attended_ref[:, pl.ds(h * head, head)] = context_sum[:, h, :].astype(bf16)

    @pl.loop(1, n)
    def _(k):
        for c in range(chunks):
            row_copy(c, k).wait_send()
        label_copy(k).wait_send()
        update_copy(k).wait_send()


def fused(
    normed_hidden,
    fresh_queries,
    fresh_key_value,
    key_value_cache,
    lengths,
    adapter_choice,
    low_rank_down,
    low_rank_up,
):
    n = lax.axis_size("wide")
    requests, model = normed_hidden.shape
    per_owner = 2 * requests // n
    kept, _, double_rank = low_rank_down.shape
    head = low_rank_up.shape[3]
    heads = fresh_queries.shape[1] // head
    context = key_value_cache.shape[1]
    slots = n * per_owner
    chunks = CHUNKS
    width = model // chunks
    bf16, f32 = jnp.bfloat16, jnp.float32
    vmem = pl.BlockSpec(memory_space=pltpu.VMEM)
    smem = pl.BlockSpec(memory_space=pltpu.SMEM)
    anywhere = pl.BlockSpec(memory_space=pl.ANY)
    return pl.pallas_call(
        functools.partial(wide_kernel, n),
        out_shape=(
            jax.ShapeDtypeStruct((requests, 2 * head), bf16),
            jax.ShapeDtypeStruct((requests, heads * head), bf16),
        ),
        in_specs=[vmem, smem, anywhere, vmem, vmem, anywhere, anywhere, vmem],
        out_specs=(vmem, vmem),
        scratch_shapes=[
            pltpu.VMEM((chunks, requests, width), bf16),
            pltpu.VMEM((requests, context, 2 * head), bf16),
            pltpu.VMEM((model, kept * double_rank), bf16),
            pltpu.VMEM((kept * double_rank, 2 * head), bf16),
            pltpu.VMEM((chunks, n, per_owner, width), bf16),
            pltpu.VMEM((chunks, n, per_owner, width), bf16),
            pltpu.VMEM((n, per_owner, 128), bf16),
            pltpu.VMEM((n, per_owner, 128), bf16),
            pltpu.VMEM((n, per_owner, 2 * head), bf16),
            pltpu.VMEM((n, per_owner, 2 * head), bf16),
            pltpu.VMEM((slots, requests), bf16),
            pltpu.VMEM((requests, slots), bf16),
            pltpu.VMEM((requests, heads, head), f32),
            pltpu.VMEM((requests, heads, head), f32),
            pltpu.VMEM((requests, heads, head), f32),
            pltpu.VMEM((requests, heads, head), f32),
            pltpu.VMEM((slots, kept * double_rank), f32),
            pltpu.SemaphoreType.DMA((chunks + kept + 1,)),
            pltpu.SemaphoreType.DMA((chunks,)),
            pltpu.SemaphoreType.DMA((chunks + 2, n)),
            pltpu.SemaphoreType.DMA((chunks + 2, n)),
        ],
        compiler_params=pltpu.CompilerParams(
            collective_id=0, has_side_effects=True, vmem_limit_bytes=56 * 1024 * 1024
        ),
    )(
        adapter_choice.reshape(1, requests),
        lengths,
        normed_hidden,
        fresh_queries,
        fresh_key_value,
        key_value_cache,
        low_rank_down,
        low_rank_up,
    )


def half_kernel(
    n,
    reps,
    ids_ref,
    lengths_ref,
    hidden_ref,
    queries_ref,
    fresh_ref,
    cache_ref,
    down_ref,
    up_ref,
    entry_ref,
    attended_ref,
    over_ref,
    hidden,
    cache,
    down,
    up,
    cross_out,
    cross_in,
    direct_out,
    forward,
    received,
    label_cross_out,
    label_cross_in,
    label_direct_out,
    label_forward,
    label_received,
    update,
    update_direct,
    update_relay,
    back_out,
    back_in,
    over_out,
    over_in,
    over_rep_out,
    over_rep_in,
    direct_place,
    direct_t,
    cross_place,
    cross_t,
    relay_place,
    relay_t,
    queries,
    context_sum,
    highest,
    total,
    project,
    load_sem,
    self_sem,
    cross_send,
    cross_recv,
    direct_send,
    direct_recv,
    forward_send,
    forward_recv,
    update_send,
    update_recv,
    relay_send,
    relay_recv,
    back_send,
    back_recv,
    over_send,
    over_recv,
    rep_send,
    rep_recv,
):
    chunks, limit, width = cross_out.shape
    inner = n // 2
    lanes = n // 4
    per_owner = direct_out.shape[2]
    kept, _, rank, head = up_ref.shape
    requests = ids_ref.shape[1]
    heads = queries.shape[1]
    slots = n * per_owner
    half_slots = inner * per_owner
    half_adapters = inner * kept
    f32, bf16 = jnp.float32, jnp.bfloat16
    nt = (((1,), (1,)), ((), ()))

    me = lax.axis_index("wide")
    rep = lax.axis_index("rep")
    plane = me // lanes
    lane = lax.rem(me, lanes)
    half = me // inner
    mine = lax.rem(me, inner)
    far = (1 - half) * 2
    is_relay = plane == 1 + half
    relay_row = (1 + half) * lanes

    def columns(c):
        return pl.ds(pl.multiple_of(c * width, width), width)

    def hidden_load(c):
        return pltpu.make_async_copy(
            hidden_ref.at[:, columns(c)], hidden.at[c], load_sem.at[c]
        )

    def down_load(g):
        return pltpu.make_async_copy(
            down_ref.at[g], down.at[:, pl.ds(g * 2 * rank, 2 * rank)], load_sem.at[chunks + g]
        )

    cache_load = pltpu.make_async_copy(cache_ref, cache, load_sem.at[chunks + kept])

    barrier = pltpu.get_barrier_semaphore()

    @pl.loop(1, n)
    def _(k):
        pl.semaphore_signal(
            barrier,
            inc=1,
            device_id={"wide": lax.rem(me + k, n)},
            device_id_type=pl.DeviceIdType.MESH,
        )

    for k in range(1, reps):
        pl.semaphore_signal(
            barrier,
            inc=1,
            device_id={"rep": lax.rem(rep + k, reps)},
            device_id_type=pl.DeviceIdType.MESH,
        )

    for c in range(chunks):
        hidden_load(c).start()
    cache_load.start()
    for g in range(kept):
        down_load(g).start()

    def remote(source, target, send_sem, recv_sem, wide):
        return pltpu.make_async_remote_copy(
            src_ref=source,
            dst_ref=target,
            send_sem=send_sem,
            recv_sem=recv_sem,
            device_id={"wide": wide},
            device_id_type=pl.DeviceIdType.MESH,
        )

    def peer(k):
        return half * inner + lax.rem(mine + k, inner)

    def cross_copy(c, b):
        source = label_cross_out if c is None else cross_out.at[c]
        target = label_cross_in.at[b] if c is None else cross_in.at[c, b]
        t = chunks if c is None else c
        return remote(
            source, target, cross_send.at[t], cross_recv.at[t, b], (2 - half) * lanes + lane
        )

    def direct_copy(c, k):
        to = peer(k)
        there = lax.rem(to, inner)
        source = label_direct_out.at[there] if c is None else direct_out.at[c, there]
        target = label_received.at[plane, lane] if c is None else received.at[c, plane, lane]
        t = chunks if c is None else c
        return remote(source, target, direct_send.at[t, k], direct_recv.at[t, k], to)

    def forward_copy(c, k, from_lane):
        to = peer(k)
        there = lax.rem(to, inner)
        source = label_forward.at[there] if c is None else forward.at[c, there]
        rows = pl.ds(far, 2)
        if c is None:
            target = label_received.at[rows, from_lane]
        else:
            target = received.at[c, rows, from_lane]
        t = chunks if c is None else c
        return remote(source, target, forward_send.at[t, k], forward_recv.at[t, from_lane], to)

    def self_copy(c):
        return pltpu.make_async_copy(
            direct_out.at[c, mine], received.at[c, plane, lane], self_sem.at[0, c]
        )

    def self_forward(c):
        return pltpu.make_async_copy(
            forward.at[c, mine], received.at[c, pl.ds(far, 2), lane], self_sem.at[1, c]
        )

    def update_copy(k):
        to = peer(k)
        return remote(
            update.at[to // lanes, lax.rem(to, lanes)],
            update_direct.at[mine],
            update_send.at[k],
            update_recv.at[k],
            to,
        )

    def relay_copy(to_lane, owner):
        return remote(
            update.at[pl.ds(far, 2), to_lane],
            update_relay.at[owner],
            relay_send.at[to_lane],
            relay_recv.at[owner],
            relay_row + to_lane,
        )

    def back_copy(b):
        return remote(
            back_out.at[b], back_in, back_send.at[b], back_recv.at[0], (far + b) * lanes + lane
        )

    def over_copy(k):
        return remote(
            over_out, over_in.at[me], over_send.at[k], over_recv.at[k], lax.rem(me + k, n)
        )

    def rep_copy(k):
        return pltpu.make_async_remote_copy(
            src_ref=over_rep_out,
            dst_ref=over_rep_in.at[rep],
            send_sem=rep_send.at[k],
            recv_sem=rep_recv.at[k],
            device_id={"rep": lax.rem(rep + k, reps)},
            device_id_type=pl.DeviceIdType.MESH,
        )

    def ranks(hit):
        size = hit.shape[1]
        before = lax.broadcasted_iota(jnp.int32, (size, size), 0)
        after = lax.broadcasted_iota(jnp.int32, (size, size), 1)
        earlier = jnp.dot(
            hit.astype(bf16),
            jnp.where(before < after, 1.0, 0.0).astype(bf16),
            preferred_element_type=f32,
        )
        return jnp.where(hit > 0.5, earlier, -1.0).astype(jnp.int32)

    def spread(hit):
        size = hit.shape[1]
        place = lax.broadcasted_iota(jnp.int32, (inner, per_owner, size), 1)
        chosen = jnp.where(place == ranks(hit)[:, None, :], 1.0, 0.0)
        return chosen.reshape(half_slots, size)

    ids = ids_ref[...]
    near = ids - half * half_adapters
    group_of = lax.broadcasted_iota(jnp.int32, (inner, 128), 1)
    first = lax.broadcasted_iota(jnp.int32, (inner, 128), 0) * kept
    grouping = jnp.where((group_of >= first) & (group_of < first + kept), 1.0, 0.0).astype(bf16)
    label_lane = lax.broadcasted_iota(jnp.int32, (128, requests), 0)
    near_flags = jnp.where(label_lane == near, 1.0, 0.0).astype(bf16)
    far_flags = jnp.where(
        label_lane == ids - (1 - half) * half_adapters, 1.0, 0.0
    ).astype(bf16)
    hit = jnp.dot(grouping, near_flags, preferred_element_type=f32)
    direct = spread(hit)
    direct_place[...] = direct.astype(bf16)
    crossing = 1.0 - jnp.sum(hit, axis=0, keepdims=True)
    cross_rank = ranks(jnp.broadcast_to(crossing, (8, requests)))[0:1, :]
    cross = jnp.where(
        lax.broadcasted_iota(jnp.int32, (limit, requests), 0) == cross_rank, 1.0, 0.0
    )
    cross_place[...] = cross.astype(bf16)
    count = jnp.sum(jnp.broadcast_to(crossing, (8, requests)), axis=1, keepdims=True)
    over = jnp.where(jnp.broadcast_to(count, (8, 128)) > limit + 0.5, 1.0, 0.0)
    over_out[...] = over
    over_in[me] = over
    label_cross_out[...] = lax.dot_general(
        cross_place[...], far_flags, nt, preferred_element_type=f32
    ).astype(bf16)
    direct_labels = lax.dot_general(
        direct_place[...], near_flags, nt, preferred_element_type=f32
    )
    label_direct_out[...] = direct_labels.astype(bf16).reshape(inner, per_owner, 128)
    label_received[plane, lane] = label_direct_out[mine]

    pl.semaphore_wait(barrier, n - 1 + reps - 1)

    b_mine = lax.rem(plane, 2)
    cross_copy(None, b_mine).start()

    @pl.loop(0, chunks)
    def _(c):
        hidden_load(c).wait()
        cross_out[c] = jnp.dot(
            cross_place[...], hidden[c], preferred_element_type=f32
        ).astype(bf16)
        cross_copy(c, b_mine).start()
        rows = jnp.dot(direct_place[...], hidden[c], preferred_element_type=f32)
        direct_out[c] = rows.astype(bf16).reshape(inner, per_owner, width)
        self_copy(c).start()

        @pl.loop(1, inner)
        def _(k):
            direct_copy(c, k).start()

    @pl.loop(1, inner)
    def _(k):
        direct_copy(None, k).start()

    @pl.loop(1, n)
    def _(k):
        over_copy(k).start()

    direct_t[...] = direct.T.astype(bf16)
    cross_t[...] = cross.T.astype(bf16)
    up[...] = jnp.zeros_like(up)
    for g in range(kept):
        for t in range(2):
            up[pl.ds((2 * g + t) * rank, rank), pl.ds(t * head, head)] = up_ref[g, t]
    project[...] = jnp.zeros_like(project)
    for h in range(heads):
        queries[:, h, :] = queries_ref[:, pl.ds(h * head, head)].astype(f32)
    cache_load.wait()
    context = cache.shape[1]
    group = 8 if requests % 8 == 0 else 1

    @pl.loop(0, requests // group)
    def _(i):
        for u in range(group):
            r = i * group + u
            scores = lax.dot_general(
                queries[r].astype(bf16),
                cache[r, :, pl.ds(0, head)],
                nt,
                preferred_element_type=f32,
            ) / math.sqrt(head)
            usable = lax.broadcasted_iota(jnp.int32, (heads, context), 1) < lengths_ref[r]
            scores = jnp.where(usable, scores, -1e30)
            top = jnp.max(scores, axis=1, keepdims=True)
            powers = jnp.where(usable, jnp.exp(scores - top), 0.0)
            highest[r] = jnp.broadcast_to(top, (heads, head))
            total[r] = jnp.broadcast_to(jnp.sum(powers, axis=1, keepdims=True), (heads, head))
            context_sum[r] = jnp.dot(
                powers.astype(bf16), cache[r, :, pl.ds(head, head)], preferred_element_type=f32
            )

    for g in range(kept):
        down_load(g).wait()

    @pl.when(is_relay)
    def _():
        for b in range(2):
            cross_copy(None, b).wait_recv()
            arrived = label_cross_in[b]
            sorted_rows = spread(
                lax.dot_general(grouping, arrived, nt, preferred_element_type=f32)
            )
            relay_place[b] = sorted_rows.astype(bf16)
            relay_t[b] = sorted_rows.T.astype(bf16)
            handed = jnp.dot(relay_place[b], arrived, preferred_element_type=f32)
            label_forward[:, b] = handed.astype(bf16).reshape(inner, per_owner, 128)

        @pl.loop(1, inner)
        def _(k):
            forward_copy(None, k, lane).start()

        label_received[pl.ds(far, 2), lane] = label_forward[mine]

    def relay(c):
        @pl.when(is_relay)
        def _():
            for b in range(2):
                cross_copy(c, b).wait_recv()
                handed = jnp.dot(relay_place[b], cross_in[c, b], preferred_element_type=f32)
                forward[c, :, b] = handed.astype(bf16).reshape(inner, per_owner, width)

            @pl.loop(1, inner)
            def _(k):
                forward_copy(c, k, lane).start()

            self_forward(c).start()

    def await_forwards(c):
        for from_lane in range(lanes):

            @pl.when(relay_row + from_lane != me)
            def _():
                forward_copy(c, 1, from_lane).wait_recv()

    def consume(c):
        self_copy(c).wait()

        @pl.loop(1, inner)
        def _(k):
            direct_copy(c, k).wait_recv()

        await_forwards(c)

        @pl.when(is_relay)
        def _():
            self_forward(c).wait()

        project[...] += jnp.dot(
            received[c].reshape(slots, width), down[columns(c), :], preferred_element_type=f32
        )

    relay(0)
    relay(1)

    @pl.loop(2, chunks)
    def _(c):
        relay(c)
        consume(c - 2)

    @pl.loop(1, n)
    def _(k):
        over_copy(k).wait_recv()

    over_rep_out[...] = jnp.max(over_in[...], axis=0)
    over_rep_in[rep] = over_rep_out[...]
    for k in range(1, reps):
        rep_copy(k).start()

    consume(chunks - 2)

    @pl.loop(1, inner)
    def _(k):
        direct_copy(None, k).wait_recv()

    await_forwards(None)
    own = lax.broadcasted_iota(jnp.int32, (128, 128), 0) - mine * kept
    select = jnp.where(own == lax.broadcasted_iota(jnp.int32, (128, 128), 1), 1.0, 0.0)
    picked = jnp.dot(
        label_received[...].reshape(slots, 128), select.astype(bf16), preferred_element_type=f32
    )
    for k in range(1, reps):
        rep_copy(k).wait_recv()
    over_ref[...] = jnp.max(over_rep_in[...], axis=0)
    consume(chunks - 1)

    masked = [
        project[:, pl.ds(g * 2 * rank, 2 * rank)] * picked[:, g : g + 1] for g in range(kept)
    ]
    computed = jnp.dot(
        jnp.concatenate(masked, axis=1).astype(bf16), up[...], preferred_element_type=f32
    )
    update[...] = computed.astype(bf16).reshape(4, lanes, per_owner, 2 * head)

    for to_lane in range(lanes):

        @pl.when(relay_row + to_lane != me)
        def _():
            relay_copy(to_lane, mine).start()

    @pl.loop(1, inner)
    def _(k):
        update_copy(k).start()

    update_direct[mine] = update[plane, lane]

    @pl.when(is_relay)
    def _():
        update_relay[mine] = update[pl.ds(far, 2), lane]

        @pl.loop(1, inner)
        def _(k):
            relay_copy(lane, lax.rem(mine + k, inner)).wait_recv()

        for b in range(2):
            back_out[b] = jnp.dot(
                relay_t[b],
                update_relay[:, b].reshape(half_slots, 2 * head),
                preferred_element_type=f32,
            ).astype(bf16)
            back_copy(b).start()

    @pl.loop(1, inner)
    def _(k):
        update_copy(k).wait_recv()

    returned = jnp.dot(
        direct_t[...],
        update_direct[...].reshape(half_slots, 2 * head),
        preferred_element_type=f32,
    )
    back_copy(0).wait_recv()
    returned = returned + jnp.dot(cross_t[...], back_in[...], preferred_element_type=f32)
    entry = (fresh_ref[...].astype(f32) + returned).astype(bf16)
    entry_ref[...] = entry
    key = entry[:, :head].astype(f32)
    value = entry[:, head:].astype(f32)
    fresh_score = jnp.sum(queries[...] * key[:, None, :], axis=2, keepdims=True) / math.sqrt(head)
    old = highest[...]
    new = jnp.maximum(old, fresh_score)
    scale = jnp.exp(old - new)
    fresh_power = jnp.exp(fresh_score - new)
    context_sum[...] = (context_sum[...] * scale + fresh_power * value[:, None, :]) / (
        total[...] * scale + fresh_power
    )
    for h in range(heads):
        attended_ref[:, pl.ds(h * head, head)] = context_sum[:, h, :].astype(bf16)

    cross_copy(None, b_mine).wait_send()

    @pl.loop(0, chunks)
    def _(c):
        cross_copy(c, b_mine).wait_send()

    @pl.loop(1, inner)
    def _(k):
        direct_copy(None, k).wait_send()
        update_copy(k).wait_send()

        @pl.loop(0, chunks)
        def _(c):
            direct_copy(c, k).wait_send()

    @pl.when(is_relay)
    def _():
        @pl.loop(1, inner)
        def _(k):
            forward_copy(None, k, lane).wait_send()

            @pl.loop(0, chunks)
            def _(c):
                forward_copy(c, k, lane).wait_send()

        for b in range(2):
            back_copy(b).wait_send()

    for to_lane in range(lanes):

        @pl.when(relay_row + to_lane != me)
        def _():
            relay_copy(to_lane, mine).wait_send()

    @pl.loop(1, n)
    def _(k):
        over_copy(k).wait_send()

    for k in range(1, reps):
        rep_copy(k).wait_send()


def by_halves(
    normed_hidden,
    fresh_queries,
    fresh_key_value,
    key_value_cache,
    lengths,
    adapter_choice,
    low_rank_down,
    low_rank_up,
):
    n = lax.axis_size("wide")
    reps = lax.axis_size("rep")
    requests, model = normed_hidden.shape
    per_owner = 2 * requests // n
    kept, _, double_rank = low_rank_down.shape
    head = low_rank_up.shape[3]
    heads = fresh_queries.shape[1] // head
    context = key_value_cache.shape[1]
    slots = n * per_owner
    inner, lanes = n // 2, n // 4
    chunks, limit = HALF_CHUNKS, 3 * requests // 4
    width = model // chunks
    bf16, f32 = jnp.bfloat16, jnp.float32
    vmem = pl.BlockSpec(memory_space=pltpu.VMEM)
    smem = pl.BlockSpec(memory_space=pltpu.SMEM)
    anywhere = pl.BlockSpec(memory_space=pl.ANY)
    dma = pltpu.SemaphoreType.DMA
    return pl.pallas_call(
        functools.partial(half_kernel, n, reps),
        out_shape=(
            jax.ShapeDtypeStruct((requests, 2 * head), bf16),
            jax.ShapeDtypeStruct((requests, heads * head), bf16),
            jax.ShapeDtypeStruct((8, 128), f32),
        ),
        in_specs=[vmem, smem, anywhere, vmem, vmem, anywhere, anywhere, vmem],
        out_specs=(vmem, vmem, vmem),
        scratch_shapes=[
            pltpu.VMEM((chunks, requests, width), bf16),
            pltpu.VMEM((requests, context, 2 * head), bf16),
            pltpu.VMEM((model, kept * double_rank), bf16),
            pltpu.VMEM((kept * double_rank, 2 * head), bf16),
            pltpu.VMEM((chunks, limit, width), bf16),
            pltpu.VMEM((chunks, 2, limit, width), bf16),
            pltpu.VMEM((chunks, inner, per_owner, width), bf16),
            pltpu.VMEM((chunks, inner, 2, per_owner, width), bf16),
            pltpu.VMEM((chunks, 4, lanes, per_owner, width), bf16),
            pltpu.VMEM((limit, 128), bf16),
            pltpu.VMEM((2, limit, 128), bf16),
            pltpu.VMEM((inner, per_owner, 128), bf16),
            pltpu.VMEM((inner, 2, per_owner, 128), bf16),
            pltpu.VMEM((4, lanes, per_owner, 128), bf16),
            pltpu.VMEM((4, lanes, per_owner, 2 * head), bf16),
            pltpu.VMEM((inner, per_owner, 2 * head), bf16),
            pltpu.VMEM((inner, 2, per_owner, 2 * head), bf16),
            pltpu.VMEM((2, limit, 2 * head), bf16),
            pltpu.VMEM((limit, 2 * head), bf16),
            pltpu.VMEM((8, 128), f32),
            pltpu.VMEM((n, 8, 128), f32),
            pltpu.VMEM((8, 128), f32),
            pltpu.VMEM((reps, 8, 128), f32),
            pltpu.VMEM((inner * per_owner, requests), bf16),
            pltpu.VMEM((requests, inner * per_owner), bf16),
            pltpu.VMEM((limit, requests), bf16),
            pltpu.VMEM((requests, limit), bf16),
            pltpu.VMEM((2, inner * per_owner, limit), bf16),
            pltpu.VMEM((2, limit, inner * per_owner), bf16),
            pltpu.VMEM((requests, heads, head), f32),
            pltpu.VMEM((requests, heads, head), f32),
            pltpu.VMEM((requests, heads, head), f32),
            pltpu.VMEM((requests, heads, head), f32),
            pltpu.VMEM((slots, kept * double_rank), f32),
            dma((chunks + kept + 1,)),
            dma((2, chunks)),
            dma((chunks + 1,)),
            dma((chunks + 1, 2)),
            dma((chunks + 1, inner)),
            dma((chunks + 1, inner)),
            dma((chunks + 1, inner)),
            dma((chunks + 1, lanes)),
            dma((inner,)),
            dma((inner,)),
            dma((lanes,)),
            dma((inner,)),
            dma((2,)),
            dma((1,)),
            dma((n,)),
            dma((n,)),
            dma((reps,)),
            dma((reps,)),
        ],
        compiler_params=pltpu.CompilerParams(
            collective_id=1, has_side_effects=True, vmem_limit_bytes=60 * 1024 * 1024
        ),
    )(
        adapter_choice.reshape(1, requests),
        lengths,
        normed_hidden,
        fresh_queries,
        fresh_key_value,
        key_value_cache,
        low_rank_down,
        low_rank_up,
    )


def device_step(*blocks):
    requests = blocks[0].shape[0]
    n = lax.axis_size("wide")
    per_owner = 2 * requests // n
    if per_owner % 16 or n != 16:
        return shards(*blocks)
    entry, attended, over = by_halves(*blocks)
    return lax.cond(over[0, 0] > 0.5, lambda: fused(*blocks), lambda: (entry, attended))


def solution(mesh):
    return jax.shard_map(
        device_step,
        mesh=mesh,
        in_specs=(
            P(("rep", "wide"), None),
            P(("rep", "wide"), None),
            P(("rep", "wide"), None),
            P(("rep", "wide"), None, None),
            P(("rep", "wide")),
            P(("rep", "wide")),
            P("wide", None, None),
            P("wide", None, None, None),
        ),
        out_specs=(P(("rep", "wide"), None), P(("rep", "wide"), None)),
        check_vma=False,
    )
```

```python
import functools
import math

import jax
import jax.numpy as jnp
from jax import lax
from jax.experimental import pallas as pl
from jax.experimental.pallas import tpu as pltpu
from jax.sharding import PartitionSpec as P

CHUNKS = 4
HALF_CHUNKS = 8


def apply_low_rank(received_rows, request_labels, low_rank_down, low_rank_up):
    kept_count = low_rank_down.shape[0]
    double_rank = low_rank_down.shape[2]
    senders = received_rows.shape[0]
    per_owner = received_rows.shape[1]
    picked = request_labels[:, :, None] == jnp.arange(kept_count)[None, None, :]
    project_input = jnp.einsum(
        "ikv,hvp->ikhp", received_rows, low_rank_down, preferred_element_type=jnp.float32
    ).astype(jnp.bfloat16)
    project_input = jnp.where(picked[:, :, :, None], project_input, jnp.zeros_like(project_input))
    project_input = project_input.reshape(senders, per_owner, kept_count, 2, double_rank // 2)
    low_rank_update = jnp.einsum(
        "uygwk,gwke->uywe", project_input, low_rank_up, preferred_element_type=jnp.float32
    )
    return low_rank_update.astype(jnp.bfloat16).reshape(senders, per_owner, -1)


def return_rows(low_rank_update):
    return lax.all_to_all(low_rank_update, "wide", split_axis=0, concat_axis=0, tiled=True)


def attend(fresh_queries, key_value_cache, lengths, entry):
    head_size = entry.shape[1] // 2
    requests = fresh_queries.shape[0]
    context = key_value_cache.shape[1]
    queries = fresh_queries.reshape(requests, -1, head_size)
    scores = jnp.einsum(
        "rqh,rch->rqc",
        queries,
        key_value_cache[:, :, :head_size],
        preferred_element_type=jnp.float32,
    ) / math.sqrt(head_size)
    usable = (jnp.arange(context, dtype=jnp.int32)[None, :] < lengths[:, None])[:, None, :]
    scores = jnp.where(usable, scores, -1e30)
    fresh_score = jnp.einsum(
        "rqh,rh->rq", queries, entry[:, :head_size], preferred_element_type=jnp.float32
    ) / math.sqrt(head_size)
    highest = jnp.maximum(jnp.max(scores, axis=2), fresh_score)
    cached_exp = jnp.where(usable, jnp.exp(scores - highest[:, :, None]), 0.0)
    fresh_exp = jnp.exp(fresh_score - highest)
    denominator = jnp.sum(cached_exp, axis=2) + fresh_exp
    cached_weight = (cached_exp / denominator[:, :, None]).astype(jnp.bfloat16)
    fresh_weight = (fresh_exp / denominator).astype(jnp.bfloat16)
    output = jnp.einsum(
        "rqc,rch->rqh",
        cached_weight,
        key_value_cache[:, :, head_size:],
        preferred_element_type=jnp.float32,
    )
    output = output + fresh_weight.astype(jnp.float32)[:, :, None] * entry[
        :, None, head_size:
    ].astype(jnp.float32)
    return output.astype(jnp.bfloat16).reshape(requests, -1)


def shards(
    normed_hidden,
    fresh_queries,
    fresh_key_value,
    key_value_cache,
    lengths,
    adapter_choice,
    low_rank_down,
    low_rank_up,
):
    devices_wide = lax.axis_size("wide")
    requests = normed_hidden.shape[0]
    per_owner = 2 * requests // devices_wide
    kept_count = low_rank_down.shape[0]
    owners = adapter_choice // kept_count
    owner_hit = owners[:, None] == jnp.arange(devices_wide, dtype=jnp.int32)[None, :]
    earlier = jnp.cumsum(owner_hit.astype(jnp.int32), axis=0) - 1
    position = jnp.sum(jnp.where(owner_hit, earlier, 0), axis=1)
    target = owners * per_owner + position
    placing = (
        target[:, None] == jnp.arange(devices_wide * per_owner, dtype=jnp.int32)[None, :]
    ).astype(jnp.bfloat16)
    packed = jnp.einsum(
        "rs,rd->sd", placing, normed_hidden, preferred_element_type=jnp.float32
    ).astype(jnp.bfloat16)
    packed = packed.reshape(devices_wide, per_owner, -1)
    every_id = lax.all_gather(adapter_choice, "wide", axis=0, tiled=True).reshape(
        devices_wide, requests
    )
    mine = every_id // kept_count == lax.axis_index("wide")
    order_mine = jnp.cumsum(mine.astype(jnp.int32), axis=1) - 1
    matched = mine[:, :, None] & (
        order_mine[:, :, None] == jnp.arange(per_owner, dtype=jnp.int32)[None, None, :]
    )
    request_labels = (
        jnp.sum(jnp.where(matched, (every_id % kept_count + 1)[:, :, None], 0), axis=1) - 1
    )
    received_rows = lax.all_to_all(packed, "wide", split_axis=0, concat_axis=0, tiled=True)
    returned_rows = return_rows(
        apply_low_rank(received_rows, request_labels, low_rank_down, low_rank_up)
    )
    flat_back = returned_rows.reshape(devices_wide * per_owner, -1)
    update_rows = jnp.einsum("rs,sh->rh", placing, flat_back, preferred_element_type=jnp.float32)
    new_entry = (fresh_key_value.astype(jnp.float32) + update_rows).astype(jnp.bfloat16)
    attended = attend(fresh_queries, key_value_cache, lengths, new_entry)
    return (new_entry, attended)

def wide_kernel(
    n,
    ids_ref,
    lengths_ref,
    hidden_ref,
    queries_ref,
    fresh_ref,
    cache_ref,
    down_ref,
    up_ref,
    entry_ref,
    attended_ref,
    hidden,
    cache,
    down,
    up,
    packed,
    received,
    labels_out,
    labels_in,
    update_out,
    update_in,
    placing,
    placing_t,
    queries,
    context_sum,
    highest,
    total,
    project,
    load_sem,
    self_sem,
    send_sem,
    recv_sem,
):
    chunks, per_owner, width = packed.shape[0], packed.shape[2], packed.shape[3]
    kept = up_ref.shape[0]
    rank = up_ref.shape[2]
    head = up_ref.shape[3]
    requests = ids_ref.shape[1]
    heads = queries.shape[1]
    slots = n * per_owner
    stride = 7 if n % 2 == 0 and n % 7 else 1
    me = lax.axis_index("wide")
    f32, bf16 = jnp.float32, jnp.bfloat16

    def columns(c):
        return pl.ds(pl.multiple_of(c * width, width), width)

    def hidden_load(c):
        return pltpu.make_async_copy(
            hidden_ref.at[:, columns(c)], hidden.at[c], load_sem.at[c]
        )

    def down_load(g):
        return pltpu.make_async_copy(
            down_ref.at[g], down.at[:, pl.ds(g * 2 * rank, 2 * rank)], load_sem.at[chunks + g]
        )

    cache_load = pltpu.make_async_copy(cache_ref, cache, load_sem.at[chunks + kept])

    for c in range(chunks):
        hidden_load(c).start()
    cache_load.start()
    for g in range(kept):
        down_load(g).start()

    barrier = pltpu.get_barrier_semaphore()

    @pl.loop(1, n)
    def _(k):
        pl.semaphore_signal(
            barrier,
            inc=1,
            device_id={"wide": lax.rem(me + k, n)},
            device_id_type=pl.DeviceIdType.MESH,
        )

    ids = ids_ref[...]
    adapter = lax.broadcasted_iota(jnp.int32, (n * kept, requests), 0)
    named = jnp.where(adapter == ids, 1.0, 0.0).astype(bf16)
    group_of = lax.broadcasted_iota(jnp.int32, (n, n * kept), 1)
    first = lax.broadcasted_iota(jnp.int32, (n, n * kept), 0) * kept
    grouping = jnp.where((group_of >= first) & (group_of < first + kept), 1.0, 0.0).astype(bf16)
    hit = jnp.dot(grouping, named, preferred_element_type=f32)
    before = lax.broadcasted_iota(jnp.int32, (requests, requests), 0)
    after = lax.broadcasted_iota(jnp.int32, (requests, requests), 1)
    earlier = jnp.dot(
        hit.astype(bf16),
        jnp.where(before < after, 1.0, 0.0).astype(bf16),
        preferred_element_type=f32,
    )
    position = jnp.where(hit > 0.5, earlier, -1.0).astype(jnp.int32)
    place = lax.broadcasted_iota(jnp.int32, (n, per_owner, requests), 1)
    chosen = jnp.where(place == position[:, None, :], 1.0, 0.0).reshape(slots, requests)
    placing[...] = chosen.astype(bf16)
    owner_row = jnp.sum(
        hit * lax.broadcasted_iota(jnp.int32, (n, requests), 0).astype(f32), axis=0, keepdims=True
    )
    within = ids - kept * owner_row.astype(jnp.int32)
    lane = lax.broadcasted_iota(jnp.int32, (128, requests), 0)
    flags = jnp.where(lane == within, 1.0, 0.0).astype(bf16)
    labels = lax.dot_general(
        placing[...], flags, (((1,), (1,)), ((), ())), preferred_element_type=f32
    )
    labels_out[...] = labels.astype(bf16).reshape(n, per_owner, 128)
    labels_in[me] = labels_out[me]

    pl.semaphore_wait(barrier, n - 1)

    def send(source, target, row, k):
        return pltpu.make_async_remote_copy(
            src_ref=source,
            dst_ref=target,
            send_sem=send_sem.at[row, k],
            recv_sem=recv_sem.at[row, k],
            device_id={"wide": lax.rem(me + k, n)},
            device_id_type=pl.DeviceIdType.MESH,
        )

    def row_copy(c, k):
        return send(packed.at[c, lax.rem(me + k, n)], received.at[c, me], c, k)

    def label_copy(k):
        return send(labels_out.at[lax.rem(me + k, n)], labels_in.at[me], chunks, k)

    def update_copy(k):
        return send(update_out.at[lax.rem(me + k, n)], update_in.at[me], chunks + 1, k)

    def self_copy(c):
        return pltpu.make_async_copy(packed.at[c, me], received.at[c, me], self_sem.at[c])

    step = min(width, 512)
    for c in range(chunks):
        hidden_load(c).wait()

        @pl.loop(0, width // step)
        def _(j):
            part = pl.ds(pl.multiple_of(j * step, step), step)
            rows = jnp.dot(placing[...], hidden[c, :, part], preferred_element_type=f32)
            packed[c, :, :, part] = rows.astype(bf16).reshape(n, per_owner, step)

        self_copy(c).start()

        @pl.loop(1, n)
        def _(j):
            row_copy(c, lax.rem(j * stride, n)).start()

        if c == 0:

            @pl.loop(1, n)
            def _(k):
                label_copy(k).start()

    placing_t[...] = chosen.T.astype(bf16)
    up[...] = jnp.zeros_like(up)
    for g in range(kept):
        for t in range(2):
            up[pl.ds((2 * g + t) * rank, rank), pl.ds(t * head, head)] = up_ref[g, t]
    for h in range(heads):
        queries[:, h, :] = queries_ref[:, pl.ds(h * head, head)].astype(f32)
    cache_load.wait()
    context = cache.shape[1]
    group = 8 if requests % 8 == 0 else 1

    @pl.loop(0, requests // group)
    def _(i):
        for u in range(group):
            r = i * group + u
            scores = lax.dot_general(
                queries[r].astype(bf16),
                cache[r, :, pl.ds(0, head)],
                (((1,), (1,)), ((), ())),
                preferred_element_type=f32,
            ) / math.sqrt(head)
            usable = lax.broadcasted_iota(jnp.int32, (heads, context), 1) < lengths_ref[r]
            scores = jnp.where(usable, scores, -1e30)
            top = jnp.max(scores, axis=1, keepdims=True)
            powers = jnp.where(usable, jnp.exp(scores - top), 0.0)
            highest[r] = jnp.broadcast_to(top, (heads, head))
            total[r] = jnp.broadcast_to(jnp.sum(powers, axis=1, keepdims=True), (heads, head))
            context_sum[r] = jnp.dot(
                powers.astype(bf16), cache[r, :, pl.ds(head, head)], preferred_element_type=f32
            )

    for g in range(kept):
        down_load(g).wait()

    for c in range(chunks):
        self_copy(c).wait()

        @pl.loop(1, n)
        def _(j):
            row_copy(c, lax.rem(j * stride, n)).wait_recv()

        product = jnp.dot(
            received[c].reshape(slots, width),
            down[pl.ds(c * width, width), :],
            preferred_element_type=f32,
        )
        if c == 0:
            project[...] = product
        else:
            project[...] += product

    @pl.loop(1, n)
    def _(k):
        label_copy(k).wait_recv()

    picked = labels_in[...].reshape(slots, 128).astype(f32)
    masked = [
        project[:, pl.ds(g * 2 * rank, 2 * rank)] * picked[:, g : g + 1] for g in range(kept)
    ]
    update = jnp.dot(
        jnp.concatenate(masked, axis=1).astype(bf16), up[...], preferred_element_type=f32
    )
    update_out[...] = update.astype(bf16).reshape(n, per_owner, 2 * head)

    @pl.loop(1, n)
    def _(k):
        update_copy(k).start()

    update_in[me] = update_out[me]

    @pl.loop(1, n)
    def _(k):
        update_copy(k).wait_recv()

    back = jnp.dot(
        placing_t[...], update_in[...].reshape(slots, 2 * head), preferred_element_type=f32
    )
    entry = (fresh_ref[...].astype(f32) + back).astype(bf16)
    entry_ref[...] = entry
    key = entry[:, :head].astype(f32)
    value = entry[:, head:].astype(f32)
    fresh_score = jnp.sum(queries[...] * key[:, None, :], axis=2, keepdims=True) / math.sqrt(head)
    old = highest[...]
    new = jnp.maximum(old, fresh_score)
    scale = jnp.exp(old - new)
    fresh_power = jnp.exp(fresh_score - new)
    context_sum[...] = (context_sum[...] * scale + fresh_power * value[:, None, :]) / (
        total[...] * scale + fresh_power
    )
    for h in range(heads):
        attended_ref[:, pl.ds(h * head, head)] = context_sum[:, h, :].astype(bf16)

    @pl.loop(1, n)
    def _(k):
        for c in range(chunks):
            row_copy(c, k).wait_send()
        label_copy(k).wait_send()
        update_copy(k).wait_send()


def fused(
    normed_hidden,
    fresh_queries,
    fresh_key_value,
    key_value_cache,
    lengths,
    adapter_choice,
    low_rank_down,
    low_rank_up,
):
    n = lax.axis_size("wide")
    requests, model = normed_hidden.shape
    per_owner = 2 * requests // n
    kept, _, double_rank = low_rank_down.shape
    head = low_rank_up.shape[3]
    heads = fresh_queries.shape[1] // head
    context = key_value_cache.shape[1]
    slots = n * per_owner
    chunks = CHUNKS
    width = model // chunks
    bf16, f32 = jnp.bfloat16, jnp.float32
    vmem = pl.BlockSpec(memory_space=pltpu.VMEM)
    smem = pl.BlockSpec(memory_space=pltpu.SMEM)
    anywhere = pl.BlockSpec(memory_space=pl.ANY)
    return pl.pallas_call(
        functools.partial(wide_kernel, n),
        out_shape=(
            jax.ShapeDtypeStruct((requests, 2 * head), bf16),
            jax.ShapeDtypeStruct((requests, heads * head), bf16),
        ),
        in_specs=[vmem, smem, anywhere, vmem, vmem, anywhere, anywhere, vmem],
        out_specs=(vmem, vmem),
        scratch_shapes=[
            pltpu.VMEM((chunks, requests, width), bf16),
            pltpu.VMEM((requests, context, 2 * head), bf16),
            pltpu.VMEM((model, kept * double_rank), bf16),
            pltpu.VMEM((kept * double_rank, 2 * head), bf16),
            pltpu.VMEM((chunks, n, per_owner, width), bf16),
            pltpu.VMEM((chunks, n, per_owner, width), bf16),
            pltpu.VMEM((n, per_owner, 128), bf16),
            pltpu.VMEM((n, per_owner, 128), bf16),
            pltpu.VMEM((n, per_owner, 2 * head), bf16),
            pltpu.VMEM((n, per_owner, 2 * head), bf16),
            pltpu.VMEM((slots, requests), bf16),
            pltpu.VMEM((requests, slots), bf16),
            pltpu.VMEM((requests, heads, head), f32),
            pltpu.VMEM((requests, heads, head), f32),
            pltpu.VMEM((requests, heads, head), f32),
            pltpu.VMEM((requests, heads, head), f32),
            pltpu.VMEM((slots, kept * double_rank), f32),
            pltpu.SemaphoreType.DMA((chunks + kept + 1,)),
            pltpu.SemaphoreType.DMA((chunks,)),
            pltpu.SemaphoreType.DMA((chunks + 2, n)),
            pltpu.SemaphoreType.DMA((chunks + 2, n)),
        ],
        compiler_params=pltpu.CompilerParams(
            collective_id=0, has_side_effects=True, vmem_limit_bytes=56 * 1024 * 1024
        ),
    )(
        adapter_choice.reshape(1, requests),
        lengths,
        normed_hidden,
        fresh_queries,
        fresh_key_value,
        key_value_cache,
        low_rank_down,
        low_rank_up,
    )


def half_kernel(
    n,
    reps,
    ids_ref,
    lengths_ref,
    hidden_ref,
    queries_ref,
    fresh_ref,
    cache_ref,
    down_ref,
    up_ref,
    entry_ref,
    attended_ref,
    over_ref,
    hidden,
    cache,
    down,
    up,
    cross_out,
    cross_in,
    direct_out,
    forward,
    received,
    labels_out,
    labels_in,
    update_out,
    update_in,
    over_rep_out,
    over_rep_in,
    placing,
    placing_t,
    cross_place,
    relay_out,
    relay_place,
    queries,
    context_sum,
    highest,
    total,
    project,
    load_sem,
    self_sem,
    cross_send,
    cross_recv,
    direct_send,
    direct_recv,
    forward_send,
    forward_recv,
    label_send,
    label_recv,
    update_send,
    update_recv,
    rep_send,
    rep_recv,
):
    chunks, limit, width = cross_out.shape
    inner = n // 2
    lanes = n // 4
    per_owner = direct_out.shape[2]
    kept, _, rank, head = up_ref.shape
    requests = ids_ref.shape[1]
    heads = queries.shape[1]
    slots = n * per_owner
    half_slots = inner * per_owner
    f32, bf16 = jnp.float32, jnp.bfloat16
    nt = (((1,), (1,)), ((), ()))

    me = lax.axis_index("wide")
    rep = lax.axis_index("rep")
    plane = me // lanes
    lane = lax.rem(me, lanes)
    half = me // inner
    mine = lax.rem(me, inner)
    far = (1 - half) * 2
    is_relay = plane == 1 + half
    relay_row = (1 + half) * lanes
    b_mine = lax.rem(plane, 2)

    def columns(c):
        return pl.ds(pl.multiple_of(c * width, width), width)

    def hidden_load(c):
        return pltpu.make_async_copy(
            hidden_ref.at[:, columns(c)], hidden.at[c], load_sem.at[c]
        )

    def down_load(g):
        return pltpu.make_async_copy(
            down_ref.at[g], down.at[:, pl.ds(g * 2 * rank, 2 * rank)], load_sem.at[chunks + g]
        )

    cache_load = pltpu.make_async_copy(cache_ref, cache, load_sem.at[chunks + kept])

    barrier = pltpu.get_barrier_semaphore()

    @pl.loop(1, n)
    def _(k):
        pl.semaphore_signal(
            barrier,
            inc=1,
            device_id={"wide": lax.rem(me + k, n)},
            device_id_type=pl.DeviceIdType.MESH,
        )

    for k in range(1, reps):
        pl.semaphore_signal(
            barrier,
            inc=1,
            device_id={"rep": lax.rem(rep + k, reps)},
            device_id_type=pl.DeviceIdType.MESH,
        )

    for c in range(chunks):
        hidden_load(c).start()
    cache_load.start()
    for g in range(kept):
        down_load(g).start()

    def remote(source, target, send_sem, recv_sem, wide):
        return pltpu.make_async_remote_copy(
            src_ref=source,
            dst_ref=target,
            send_sem=send_sem,
            recv_sem=recv_sem,
            device_id={"wide": wide},
            device_id_type=pl.DeviceIdType.MESH,
        )

    def peer(k):
        return half * inner + lax.rem(mine + k, inner)

    def matrix_copy(b):
        return remote(
            relay_out,
            relay_place.at[b],
            cross_send.at[chunks],
            cross_recv.at[chunks, b],
            (2 - half) * lanes + lane,
        )

    def cross_copy(c, b):
        return remote(
            cross_out.at[c],
            cross_in.at[c, b],
            cross_send.at[c],
            cross_recv.at[c, b],
            (2 - half) * lanes + lane,
        )

    def direct_copy(c, k):
        to = peer(k)
        return remote(
            direct_out.at[c, lax.rem(to, inner)],
            received.at[c, plane, lane],
            direct_send.at[c, k],
            direct_recv.at[c, k],
            to,
        )

    def forward_copy(c, k, from_lane):
        to = peer(k)
        return remote(
            forward.at[c, lax.rem(to, inner)],
            received.at[c, pl.ds(far, 2), from_lane],
            forward_send.at[c, k],
            forward_recv.at[c, from_lane],
            to,
        )

    def label_copy(k):
        to = lax.rem(me + k, n)
        return remote(labels_out.at[to], labels_in.at[me], label_send.at[k], label_recv.at[k], to)

    def update_copy(k):
        to = lax.rem(me + k, n)
        return remote(
            update_out.at[to], update_in.at[me], update_send.at[k], update_recv.at[k], to
        )

    def self_copy(c):
        return pltpu.make_async_copy(
            direct_out.at[c, mine], received.at[c, plane, lane], self_sem.at[0, c]
        )

    def self_forward(c):
        return pltpu.make_async_copy(
            forward.at[c, mine], received.at[c, pl.ds(far, 2), lane], self_sem.at[1, c]
        )

    def rep_copy(k):
        return pltpu.make_async_remote_copy(
            src_ref=over_rep_out,
            dst_ref=over_rep_in.at[rep],
            send_sem=rep_send.at[k],
            recv_sem=rep_recv.at[k],
            device_id={"rep": lax.rem(rep + k, reps)},
            device_id_type=pl.DeviceIdType.MESH,
        )

    def ranks(hit):
        before = lax.broadcasted_iota(jnp.int32, (requests, requests), 0)
        after = lax.broadcasted_iota(jnp.int32, (requests, requests), 1)
        earlier = jnp.dot(
            hit.astype(bf16),
            jnp.where(before < after, 1.0, 0.0).astype(bf16),
            preferred_element_type=f32,
        )
        return jnp.where(hit > 0.5, earlier, -1.0).astype(jnp.int32)

    ids = ids_ref[...]
    adapter = lax.broadcasted_iota(jnp.int32, (n * kept, requests), 0)
    named = jnp.where(adapter == ids, 1.0, 0.0).astype(bf16)
    group_of = lax.broadcasted_iota(jnp.int32, (n, n * kept), 1)
    first = lax.broadcasted_iota(jnp.int32, (n, n * kept), 0) * kept
    grouping = jnp.where((group_of >= first) & (group_of < first + kept), 1.0, 0.0).astype(bf16)
    hit = jnp.dot(grouping, named, preferred_element_type=f32)
    place = lax.broadcasted_iota(jnp.int32, (n, per_owner, requests), 1)
    chosen = jnp.where(place == ranks(hit)[:, None, :], 1.0, 0.0).reshape(slots, requests)
    placing[...] = chosen.astype(bf16)
    owner = lax.broadcasted_iota(jnp.int32, (n, requests), 0)
    across = jnp.where((owner >= (1 - half) * inner) & (owner < (2 - half) * inner), hit, 0.0)
    crossing = jnp.broadcast_to(jnp.sum(across, axis=0, keepdims=True), (8, requests))
    cross = jnp.where(
        lax.broadcasted_iota(jnp.int32, (limit, requests), 0) == ranks(crossing)[0:1, :], 1.0, 0.0
    )
    cross_place[...] = cross.astype(bf16)
    near_rows = pl.ds(pl.multiple_of(half * half_slots, half_slots), half_slots)
    far_rows = pl.ds(pl.multiple_of((1 - half) * half_slots, half_slots), half_slots)
    relay_out[...] = lax.dot_general(
        placing[far_rows, :], cross_place[...], nt, preferred_element_type=f32
    ).astype(bf16)

    pl.semaphore_wait(barrier, n - 1 + reps - 1)
    matrix_copy(b_mine).start()

    @pl.loop(0, chunks)
    def _(c):
        hidden_load(c).wait()
        rows = jnp.dot(placing[near_rows, :], hidden[c], preferred_element_type=f32)
        direct_out[c] = rows.astype(bf16).reshape(inner, per_owner, width)
        self_copy(c).start()

        @pl.loop(1, inner)
        def _(k):
            direct_copy(c, k).start()

        cross_out[c] = jnp.dot(
            cross_place[...], hidden[c], preferred_element_type=f32
        ).astype(bf16)
        cross_copy(c, b_mine).start()

    owner_row = jnp.sum(hit * owner.astype(f32), axis=0, keepdims=True)
    within = ids - kept * owner_row.astype(jnp.int32)
    label_lane = lax.broadcasted_iota(jnp.int32, (128, requests), 0)
    flags = jnp.where(label_lane == within, 1.0, 0.0).astype(bf16)
    labels = lax.dot_general(placing[...], flags, nt, preferred_element_type=f32)
    count = jnp.sum(crossing, axis=1, keepdims=True)[0:1, :]
    over = jnp.where(count > limit + 0.5, 1.0, 0.0)
    last = lax.broadcasted_iota(jnp.int32, (slots, 128), 1) == 127
    labels = jnp.where(last, jnp.broadcast_to(over, (slots, 128)), labels)
    labels_out[...] = labels.astype(bf16).reshape(n, per_owner, 128)
    labels_in[me] = labels_out[me]

    @pl.loop(1, n)
    def _(k):
        label_copy(k).start()

    placing_t[...] = chosen.T.astype(bf16)
    up[...] = jnp.zeros_like(up)
    for g in range(kept):
        for t in range(2):
            up[pl.ds((2 * g + t) * rank, rank), pl.ds(t * head, head)] = up_ref[g, t]
    project[...] = jnp.zeros_like(project)
    for h in range(heads):
        queries[:, h, :] = queries_ref[:, pl.ds(h * head, head)].astype(f32)
    cache_load.wait()
    context = cache.shape[1]
    group = 8
    batches = requests // group // chunks

    for g in range(kept):
        down_load(g).wait()

    @pl.when(is_relay)
    def _():
        for b in range(2):
            matrix_copy(b).wait_recv()

    def relay(c):
        @pl.when(is_relay)
        def _():
            for b in range(2):
                cross_copy(c, b).wait_recv()
                handed = jnp.dot(relay_place[b], cross_in[c, b], preferred_element_type=f32)
                forward[c, :, b] = handed.astype(bf16).reshape(inner, per_owner, width)

            @pl.loop(1, inner)
            def _(k):
                forward_copy(c, k, lane).start()

            self_forward(c).start()

    def await_forwards(c):
        for from_lane in range(lanes):

            @pl.when(relay_row + from_lane != me)
            def _():
                forward_copy(c, 1, from_lane).wait_recv()

    def consume(c):
        self_copy(c).wait()

        @pl.loop(1, inner)
        def _(k):
            direct_copy(c, k).wait_recv()

        await_forwards(c)

        @pl.when(is_relay)
        def _():
            self_forward(c).wait()

        project[...] += jnp.dot(
            received[c].reshape(slots, width), down[columns(c), :], preferred_element_type=f32
        )

    def attend_slice(c):
        @pl.loop(c * batches, (c + 1) * batches)
        def _(i):
            for u in range(group):
                r = i * group + u
                scores = lax.dot_general(
                    queries[r].astype(bf16),
                    cache[r, :, pl.ds(0, head)],
                    nt,
                    preferred_element_type=f32,
                ) / math.sqrt(head)
                usable = lax.broadcasted_iota(jnp.int32, (heads, context), 1) < lengths_ref[r]
                scores = jnp.where(usable, scores, -1e30)
                top = jnp.max(scores, axis=1, keepdims=True)
                powers = jnp.where(usable, jnp.exp(scores - top), 0.0)
                highest[r] = jnp.broadcast_to(top, (heads, head))
                total[r] = jnp.broadcast_to(jnp.sum(powers, axis=1, keepdims=True), (heads, head))
                context_sum[r] = jnp.dot(
                    powers.astype(bf16), cache[r, :, pl.ds(head, head)], preferred_element_type=f32
                )

    relay(0)
    attend_slice(0)
    relay(1)
    attend_slice(1)

    @pl.loop(2, chunks)
    def _(c):
        relay(c)
        attend_slice(c)
        consume(c - 2)

    @pl.loop(1, n)
    def _(k):
        label_copy(k).wait_recv()

    picked = labels_in[...].reshape(slots, 128).astype(f32)
    over_rep_out[...] = jnp.broadcast_to(jnp.max(picked, axis=0, keepdims=True), (8, 128))
    over_rep_in[rep] = over_rep_out[...]
    for k in range(1, reps):
        rep_copy(k).start()

    consume(chunks - 2)
    for k in range(1, reps):
        rep_copy(k).wait_recv()
    over_ref[0, 0] = jnp.max(over_rep_in[:, :, 127:128])
    consume(chunks - 1)

    masked = [
        project[:, pl.ds(g * 2 * rank, 2 * rank)] * picked[:, g : g + 1] for g in range(kept)
    ]
    computed = jnp.dot(
        jnp.concatenate(masked, axis=1).astype(bf16), up[...], preferred_element_type=f32
    )
    update_out[...] = computed.astype(bf16).reshape(n, per_owner, 2 * head)

    @pl.loop(1, n)
    def _(k):
        update_copy(k).start()

    update_in[me] = update_out[me]

    @pl.loop(1, n)
    def _(k):
        update_copy(k).wait_recv()

    returned = jnp.dot(
        placing_t[...], update_in[...].reshape(slots, 2 * head), preferred_element_type=f32
    )
    entry = (fresh_ref[...].astype(f32) + returned).astype(bf16)
    entry_ref[...] = entry
    key = entry[:, :head].astype(f32)
    value = entry[:, head:].astype(f32)
    fresh_score = jnp.sum(queries[...] * key[:, None, :], axis=2, keepdims=True) / math.sqrt(head)
    old = highest[...]
    new = jnp.maximum(old, fresh_score)
    scale = jnp.exp(old - new)
    fresh_power = jnp.exp(fresh_score - new)
    context_sum[...] = (context_sum[...] * scale + fresh_power * value[:, None, :]) / (
        total[...] * scale + fresh_power
    )
    for h in range(heads):
        attended_ref[:, pl.ds(h * head, head)] = context_sum[:, h, :].astype(bf16)

    matrix_copy(b_mine).wait_send()

    @pl.loop(0, chunks)
    def _(c):
        cross_copy(c, b_mine).wait_send()

        @pl.loop(1, inner)
        def _(k):
            direct_copy(c, k).wait_send()

    @pl.when(is_relay)
    def _():
        @pl.loop(0, chunks)
        def _(c):
            @pl.loop(1, inner)
            def _(k):
                forward_copy(c, k, lane).wait_send()

    @pl.loop(1, n)
    def _(k):
        label_copy(k).wait_send()
        update_copy(k).wait_send()

    for k in range(1, reps):
        rep_copy(k).wait_send()


def by_halves(
    normed_hidden,
    fresh_queries,
    fresh_key_value,
    key_value_cache,
    lengths,
    adapter_choice,
    low_rank_down,
    low_rank_up,
):
    n = lax.axis_size("wide")
    reps = lax.axis_size("rep")
    requests, model = normed_hidden.shape
    per_owner = 2 * requests // n
    kept, _, double_rank = low_rank_down.shape
    head = low_rank_up.shape[3]
    heads = fresh_queries.shape[1] // head
    context = key_value_cache.shape[1]
    slots = n * per_owner
    inner, lanes = n // 2, n // 4
    chunks, limit = HALF_CHUNKS, 3 * requests // 4
    width = model // chunks
    bf16, f32 = jnp.bfloat16, jnp.float32
    vmem = pl.BlockSpec(memory_space=pltpu.VMEM)
    smem = pl.BlockSpec(memory_space=pltpu.SMEM)
    anywhere = pl.BlockSpec(memory_space=pl.ANY)
    dma = pltpu.SemaphoreType.DMA
    return pl.pallas_call(
        functools.partial(half_kernel, n, reps),
        out_shape=(
            jax.ShapeDtypeStruct((requests, 2 * head), bf16),
            jax.ShapeDtypeStruct((requests, heads * head), bf16),
            jax.ShapeDtypeStruct((1, 1), f32),
        ),
        in_specs=[vmem, smem, anywhere, vmem, vmem, anywhere, anywhere, vmem],
        out_specs=(vmem, vmem, smem),
        scratch_shapes=[
            pltpu.VMEM((chunks, requests, width), bf16),
            pltpu.VMEM((requests, context, 2 * head), bf16),
            pltpu.VMEM((model, kept * double_rank), bf16),
            pltpu.VMEM((kept * double_rank, 2 * head), bf16),
            pltpu.VMEM((chunks, limit, width), bf16),
            pltpu.VMEM((chunks, 2, limit, width), bf16),
            pltpu.VMEM((chunks, inner, per_owner, width), bf16),
            pltpu.VMEM((chunks, inner, 2, per_owner, width), bf16),
            pltpu.VMEM((chunks, 4, lanes, per_owner, width), bf16),
            pltpu.VMEM((n, per_owner, 128), bf16),
            pltpu.VMEM((n, per_owner, 128), bf16),
            pltpu.VMEM((n, per_owner, 2 * head), bf16),
            pltpu.VMEM((n, per_owner, 2 * head), bf16),
            pltpu.VMEM((8, 128), f32),
            pltpu.VMEM((reps, 8, 128), f32),
            pltpu.VMEM((slots, requests), bf16),
            pltpu.VMEM((requests, slots), bf16),
            pltpu.VMEM((limit, requests), bf16),
            pltpu.VMEM((inner * per_owner, limit), bf16),
            pltpu.VMEM((2, inner * per_owner, limit), bf16),
            pltpu.VMEM((requests, heads, head), f32),
            pltpu.VMEM((requests, heads, head), f32),
            pltpu.VMEM((requests, heads, head), f32),
            pltpu.VMEM((requests, heads, head), f32),
            pltpu.VMEM((slots, kept * double_rank), f32),
            dma((chunks + kept + 1,)),
            dma((2, chunks)),
            dma((chunks + 1,)),
            dma((chunks + 1, 2)),
            dma((chunks, inner)),
            dma((chunks, inner)),
            dma((chunks, inner)),
            dma((chunks, lanes)),
            dma((n,)),
            dma((n,)),
            dma((n,)),
            dma((n,)),
            dma((reps,)),
            dma((reps,)),
        ],
        compiler_params=pltpu.CompilerParams(
            collective_id=1, has_side_effects=True, vmem_limit_bytes=60 * 1024 * 1024
        ),
    )(
        adapter_choice.reshape(1, requests),
        lengths,
        normed_hidden,
        fresh_queries,
        fresh_key_value,
        key_value_cache,
        low_rank_down,
        low_rank_up,
    )


def device_step(*blocks):
    requests = blocks[0].shape[0]
    n = lax.axis_size("wide")
    per_owner = 2 * requests // n
    if per_owner % 16 or n != 16:
        return shards(*blocks)
    entry, attended, over = by_halves(*blocks)
    return lax.cond(over[0, 0] > 0.5, lambda: fused(*blocks), lambda: (entry, attended))


def solution(mesh):
    return jax.shard_map(
        device_step,
        mesh=mesh,
        in_specs=(
            P(("rep", "wide"), None),
            P(("rep", "wide"), None),
            P(("rep", "wide"), None),
            P(("rep", "wide"), None, None),
            P(("rep", "wide")),
            P(("rep", "wide")),
            P("wide", None, None),
            P("wide", None, None, None),
        ),
        out_specs=(P(("rep", "wide"), None), P(("rep", "wide"), None)),
        check_vma=False,
    )
```
